32 devices in a mesh: group: 2 (over x), sector: 16 (over z, y, core).
Axes of the slice: x: 2, y: 2, z: 4, core: 2. Of those that a mesh axis runs over, the one named last changes fastest.
Arguments:
- wave: bfloat16 [32, 16, 256, 256], P(('group', 'sector')), parts along dimension 0, may hold values from -6 to 6
- left_ops: bfloat16 [384, 256, 256], P(('group', 'sector')), parts along dimension 0, may hold values from -0.375 to 0.375
- right_ops: bfloat16 [384, 256, 256], P(('group', 'sector')), parts along dimension 0, may hold values from -0.375 to 0.375
- deltas: int32 [384], P(('group', 'sector')), parts along dimension 0, may hold values from -1 to 1, as said below
- counts: int32 [32], P(('group', 'sector')), parts along dimension 0, may hold values from 2 to 12, as said below
Outputs:
- sigma: bfloat16 [32, 16, 256, 256], P(('group', 'sector')), parts along dimension 0
The draws below stay inside these ranges and needn't reach their ends.
There are 2 independent parts, one for each index of `group`. The reference program is written for one: setup_inputs(seed, part) draws one part's arguments, and reference() takes and returns one part's arrays. A program takes and returns all parts, laid end to end along the dimension named above; each array names one. Nothing has to cross between parts.
Inputs may be any that keep to these rules, and one draw needn't show every extreme that they name: `counts`: some sector has exactly 12 live slots in every draw; slots at or beyond a sector's count are unused. Every sector has 2 or more live slots. In each aligned pair of sectors 2i and 2i + 1 at most one has more than 6 live slots, and every other sector has 2 or 3 live slots. `deltas`: slot 0 of every sector reads the sector below it (offset -1) and slot 1 the sector above it (offset +1).
All inputs are finite; a program needn't handle non-finite values.
Results may differ from the reference program's by a relative error of at most 0.0049.
Values may be sent and summed in bfloat16 or wider, within the bound.
A program may use at most 64 MiB of HBM per device.

```python
import jax
import jax.numpy as jnp
from jax import lax

M = 256
ROOTS = 16
SLOTS = 12
SECTORS = 16


def draw_deltas(key, part):
    random_part = jax.random.randint(jax.random.fold_in(key, 11), (SECTORS * SLOTS,), -1, 2)
    slot_ids = jnp.arange(SECTORS * SLOTS, dtype=jnp.int32) % SLOTS
    values = jnp.where(slot_ids == 0, -1, jnp.where(slot_ids == 1, 1, random_part))
    return values.astype(jnp.int32)


def draw_counts(key, part):
    first_key, second_key, third_key, fourth_key = jax.random.split(key, 4)
    pairs_total = SECTORS // 2
    lighter = jax.random.randint(first_key, (SECTORS,), 2, max(2, SLOTS // 4) + 1)
    loaded_pair = jax.random.randint(second_key, (pairs_total,), 0, 4) != 0
    forced = jax.random.randint(third_key, (), 0, pairs_total)
    loaded_pair = loaded_pair.at[forced].set(True)
    member = jax.random.randint(fourth_key, (pairs_total,), 0, 2)
    sector_ids = jnp.arange(SECTORS, dtype=jnp.int32)
    pair_of = sector_ids // 2
    heavy = jnp.logical_and(loaded_pair[pair_of], sector_ids % 2 == member[pair_of])
    values = jnp.where(heavy, SLOTS, lighter)
    return values.astype(jnp.int32)


def steps_of(key, extent, cuts, smallest, top_value):
    def one(position, blocks):
        draws = jax.random.uniform(jax.random.fold_in(jax.random.fold_in(key, 6), position), (blocks,), jnp.float32, smallest / len(cuts), top_value / len(cuts))
        return jnp.repeat(jnp.exp(draws), extent[position] // blocks).reshape((-1,) + (1,) * (len(extent) - position - 1))

    gain = one(*cuts[0])
    for cut in cuts[1:]:
        gain = gain * one(*cut)
    return gain


def gaussian(stream_key, extent, deviation, reach, shards=(), kind=jnp.bfloat16):
    values = deviation * jax.random.normal(stream_key, extent, jnp.float32)
    if shards:
        values = values * steps_of(stream_key, extent, shards, -0.22, 0.18)
    return jnp.clip(values, -reach, reach).astype(kind)


def setup_inputs(seed: int = 0, part: int = 0) -> dict:
    streams_of = jax.random.split(jax.random.key(seed), 6)
    part_keys = jax.random.split(jax.random.fold_in(streams_of[5], part), 6)
    wave = gaussian(part_keys[0], (SECTORS, ROOTS, M, M), 1.0, 6.0, ((0, 16),))
    left_ops = gaussian(part_keys[1], (SECTORS * SLOTS, M, M), M ** -0.5, 0.375, ((0, 16),))
    right_ops = gaussian(part_keys[2], (SECTORS * SLOTS, M, M), M ** -0.5, 0.375, ((0, 16),))
    deltas = draw_deltas(jax.random.fold_in(jax.random.fold_in(streams_of[5], part), 71), part)
    counts = draw_counts(jax.random.fold_in(jax.random.fold_in(streams_of[5], part), 71), part)
    return {"wave": wave, "left_ops": left_ops, "right_ops": right_ops, "deltas": deltas, "counts": counts}


def reference(wave, left_ops, right_ops, deltas, counts):
    border = jnp.zeros((1, ROOTS, M, M), jnp.bfloat16)
    padded = jnp.concatenate([border, wave, border], 0)

    def one_sector(sector):
        def add_pair(slot_index, running):
            pair = (sector * SLOTS + slot_index).astype(jnp.int32)
            source = (sector + 1 + deltas[pair]).astype(jnp.int32)
            source_block = lax.dynamic_index_in_dim(padded, source, 0, keepdims=False)
            left_op = lax.dynamic_index_in_dim(left_ops, pair, 0, keepdims=False)
            right_op = lax.dynamic_index_in_dim(right_ops, pair, 0, keepdims=False)
            mixed = jnp.einsum("ij,rjk->rik", left_op.astype(jnp.float32), source_block.astype(jnp.float32)).astype(jnp.bfloat16)
            return running + jnp.einsum("rik,lk->ril", mixed.astype(jnp.float32), right_op.astype(jnp.float32))

        running = lax.fori_loop(jnp.int32(0), counts[sector].astype(jnp.int32), add_pair, jnp.zeros((ROOTS, M, M), jnp.float32))
        return running.astype(jnp.bfloat16)

    return lax.map(one_sector, jnp.arange(SECTORS, dtype=jnp.int32))
```

```python
import functools

import jax
import jax.numpy as jnp
from jax import lax
from jax.experimental import pallas as pl
from jax.experimental.pallas import tpu as pltpu
from jax.sharding import PartitionSpec as P

MESH = pl.DeviceIdType.MESH


def kernel(
    sectors, counts_ref, deltas_ref, wave_ref, left_ref, right_ref, out_ref,
    own, low, high, left, right, right_t, stage, mixed, result,
    send_sem, low_sem, high_sem, own_sem, op_sem, out_sem,
):
    roots, width = own.shape[0], own.shape[1]
    slots = left.shape[0]
    me = lax.axis_index("sector")
    has_low, has_high = me > 0, me < sectors - 1

    barrier = pltpu.get_barrier_semaphore()

    @pl.when(has_low)
    def _():
        pl.semaphore_signal(barrier, inc=1, device_id={"sector": me - 1}, device_id_type=MESH)

    @pl.when(has_high)
    def _():
        pl.semaphore_signal(barrier, inc=1, device_id={"sector": me + 1}, device_id_type=MESH)

    left_copy = pltpu.make_async_copy(left_ref, left, op_sem.at[0])
    right_copy = pltpu.make_async_copy(right_ref, right, op_sem.at[1])
    own_copy = pltpu.make_async_copy(wave_ref, own, own_sem)
    left_copy.start()
    right_copy.start()
    own_copy.start()

    pl.semaphore_wait(barrier, has_low.astype(jnp.int32) + has_high.astype(jnp.int32))

    def up(root):
        return pltpu.make_async_remote_copy(
            src_ref=wave_ref.at[root], dst_ref=low.at[root],
            send_sem=send_sem.at[0, root], recv_sem=low_sem.at[root],
            device_id={"sector": me + 1}, device_id_type=MESH,
        )

    def down(root):
        return pltpu.make_async_remote_copy(
            src_ref=wave_ref.at[root], dst_ref=high.at[root],
            send_sem=send_sem.at[1, root], recv_sem=high_sem.at[root],
            device_id={"sector": me - 1}, device_id_type=MESH,
        )

    @pl.loop(0, roots)
    def _(root):
        @pl.when(has_high)
        def _():
            up(root).start()

        @pl.when(has_low)
        def _():
            down(root).start()

    @pl.when(jnp.logical_not(has_low))
    def _():
        low[...] = jnp.zeros_like(low)

    @pl.when(jnp.logical_not(has_high))
    def _():
        high[...] = jnp.zeros_like(high)

    left_copy.wait()
    right_copy.wait()
    count = counts_ref[0]

    @pl.loop(0, slots)
    def _(slot):
        live = jnp.where(slot < count, 1.0, 0.0).astype(jnp.float32)
        left[slot] = (left[slot].astype(jnp.float32) * live).astype(left.dtype)
        right_t[pl.ds(pl.multiple_of(slot * width, width), width), :] = right[slot].T

    own_copy.wait()

    def out_copy(root, slot):
        return pltpu.make_async_copy(result.at[slot], out_ref.at[root], out_sem.at[slot])

    @pl.loop(0, roots)
    def _(root):
        @pl.when(has_low)
        def _():
            up(root).wait_recv()

        @pl.when(has_high)
        def _():
            down(root).wait_recv()

        stage[0] = low[root]
        stage[1] = own[root]
        stage[2] = high[root]
        for slot in range(slots):
            source = stage[deltas_ref[slot] + 1]
            mixed[:, slot * width:(slot + 1) * width] = jnp.dot(
                left[slot], source, preferred_element_type=jnp.float32
            ).astype(mixed.dtype)
        total = jnp.dot(mixed[...], right_t[...], preferred_element_type=jnp.float32)
        now = lax.rem(root, 2)

        @pl.when(root >= 2)
        def _():
            out_copy(root - 2, now).wait()

        result[now] = total.astype(result.dtype)
        out_copy(root, now).start()

    for root in (roots - 2, roots - 1):
        out_copy(root, root % 2).wait()

    @pl.loop(0, roots)
    def _(root):
        @pl.when(has_high)
        def _():
            up(root).wait_send()

        @pl.when(has_low)
        def _():
            down(root).wait_send()


def on_device(sectors, wave, left_ops, right_ops, deltas, counts):
    wave = wave[0]
    roots, width = wave.shape[0], wave.shape[1]
    slots = left_ops.shape[0]
    block = (roots, width, width)
    bf16 = wave.dtype
    flops = 4 * roots * slots * width**3
    sigma = pl.pallas_call(
        functools.partial(kernel, sectors),
        out_shape=jax.ShapeDtypeStruct(block, bf16),
        in_specs=[pl.BlockSpec(memory_space=pltpu.SMEM)] * 2 + [pl.BlockSpec(memory_space=pl.ANY)] * 3,
        out_specs=pl.BlockSpec(memory_space=pl.ANY),
        scratch_shapes=[
            pltpu.VMEM(block, bf16),
            pltpu.VMEM(block, bf16),
            pltpu.VMEM(block, bf16),
            pltpu.VMEM((slots, width, width), bf16),
            pltpu.VMEM((slots, width, width), bf16),
            pltpu.VMEM((slots * width, width), bf16),
            pltpu.VMEM((3, width, width), bf16),
            pltpu.VMEM((width, slots * width), bf16),
            pltpu.VMEM((2, width, width), bf16),
            pltpu.SemaphoreType.DMA((2, roots)),
            pltpu.SemaphoreType.DMA((roots,)),
            pltpu.SemaphoreType.DMA((roots,)),
            pltpu.SemaphoreType.DMA,
            pltpu.SemaphoreType.DMA((2,)),
            pltpu.SemaphoreType.DMA((2,)),
        ],
        compiler_params=pltpu.CompilerParams(
            collective_id=0, has_side_effects=True, vmem_limit_bytes=60 * 2**20
        ),
        cost_estimate=pl.CostEstimate(flops=flops, bytes_accessed=7 * 2**20, transcendentals=0),
    )(counts, deltas, wave, left_ops, right_ops)
    return sigma[None]


def solution(mesh):
    return jax.shard_map(
        functools.partial(on_device, mesh.shape["sector"]),
        mesh=mesh,
        in_specs=(
            P(("group", "sector"), None, None, None),
            P(("group", "sector"), None, None),
            P(("group", "sector"), None, None),
            P(("group", "sector")),
            P(("group", "sector")),
        ),
        out_specs=P(("group", "sector"), None, None, None),
        check_vma=False,
    )
```

```python
import functools

import jax
import jax.numpy as jnp
from jax import lax
from jax.experimental import pallas as pl
from jax.experimental.pallas import tpu as pltpu
from jax.sharding import PartitionSpec as P

MESH = pl.DeviceIdType.MESH


def kernel(
    sectors, counts_ref, deltas_ref, wave_ref, left_ref, right_ref, out_ref,
    own, low, high, passing, left, right, right_t, stage, mixed, result,
    send_sem, low_sem, high_sem, passing_sem, forward_sem, own_sem, op_sem, out_sem,
):
    roots, width = own.shape[0], own.shape[1]
    slots = left.shape[0]
    me = lax.axis_index("sector")
    has_low, has_high = me > 0, me < sectors - 1

    rows = sectors // 4 if sectors == 16 else 0
    row, place = lax.div(me, 4), lax.rem(me, 4)
    above, below = row < rows - 1, jnp.logical_and(row > 0, row < rows)
    up_source = jnp.logical_and(place == 3, above)
    up_relay = jnp.logical_and(place == 1, above)
    down_source = jnp.logical_and(place == 0, below)
    down_relay = jnp.logical_and(place == 2, below)
    up_share = lax.div(roots * (rows - 1 - row), max(rows, 1))
    down_share = lax.div(roots * row, max(rows, 1))
    up_detour = jnp.where(up_source, up_share, 0)
    down_detour = jnp.where(down_source, down_share, 0)
    forwards = jnp.where(up_relay, up_share, jnp.where(down_relay, down_share, 0))
    ahead = jnp.where(up_relay, me + 3, jnp.where(down_relay, me - 3, me))

    partners = [(has_low, me - 1), (has_high, me + 1)]
    if rows:
        partners += [
            (up_source, me - 2), (up_source, me + 3),
            (down_source, me + 2), (down_source, me - 3),
            (up_relay, me + 2), (up_relay, me + 3),
            (down_relay, me - 2), (down_relay, me - 3),
        ]
    barrier = pltpu.get_barrier_semaphore()
    for present, partner in partners:
        @pl.when(present)
        def _(partner=partner):
            pl.semaphore_signal(barrier, inc=1, device_id={"sector": partner}, device_id_type=MESH)

    left_copy = pltpu.make_async_copy(left_ref, left, op_sem.at[0])
    right_copy = pltpu.make_async_copy(right_ref, right, op_sem.at[1])
    own_copy = pltpu.make_async_copy(wave_ref, own, own_sem)
    left_copy.start()
    right_copy.start()
    own_copy.start()
    pl.semaphore_wait(barrier, sum(present.astype(jnp.int32) for present, _ in partners))

    def up(root):
        return pltpu.make_async_remote_copy(
            src_ref=wave_ref.at[root], dst_ref=low.at[root],
            send_sem=send_sem.at[0, root], recv_sem=low_sem.at[root],
            device_id={"sector": me + 1}, device_id_type=MESH,
        )

    def down(root):
        return pltpu.make_async_remote_copy(
            src_ref=wave_ref.at[root], dst_ref=high.at[root],
            send_sem=send_sem.at[1, root], recv_sem=high_sem.at[root],
            device_id={"sector": me - 1}, device_id_type=MESH,
        )

    def aside(root, step, way, corner):
        return pltpu.make_async_remote_copy(
            src_ref=wave_ref.at[root], dst_ref=passing.at[step],
            send_sem=send_sem.at[way, root], recv_sem=passing_sem.at[step],
            device_id={"sector": corner}, device_id_type=MESH,
        )

    def forward(step, target, target_sem):
        root = roots - forwards + step
        return pltpu.make_async_remote_copy(
            src_ref=passing.at[step], dst_ref=target.at[root],
            send_sem=forward_sem.at[step], recv_sem=target_sem.at[root],
            device_id={"sector": ahead}, device_id_type=MESH,
        )

    @pl.loop(0, roots)
    def _(step):
        @pl.when(jnp.logical_and(has_high, step < roots - up_detour))
        def _():
            up(step).start()

        @pl.when(jnp.logical_and(has_low, step < roots - down_detour))
        def _():
            down(step).start()

        if rows:
            @pl.when(step < up_detour)
            def _():
                aside(roots - up_detour + step, step, 0, me - 2).start()

            @pl.when(step < down_detour)
            def _():
                aside(roots - down_detour + step, step, 1, me + 2).start()

    @pl.when(jnp.logical_not(has_low))
    def _():
        low[...] = jnp.zeros_like(low)

    @pl.when(jnp.logical_not(has_high))
    def _():
        high[...] = jnp.zeros_like(high)

    left_copy.wait()
    right_copy.wait()
    count = counts_ref[0]

    @pl.loop(0, slots)
    def _(slot):
        live = jnp.where(slot < count, 1.0, 0.0).astype(jnp.float32)
        left[slot] = (left[slot].astype(jnp.float32) * live).astype(left.dtype)
        right_t[pl.ds(pl.multiple_of(slot * width, width), width), :] = right[slot].T

    own_copy.wait()

    def out_copy(root, slot):
        return pltpu.make_async_copy(result.at[slot], out_ref.at[root], out_sem.at[slot])

    @pl.loop(0, roots)
    def _(root):
        @pl.when(has_low)
        def _():
            up(root).wait_recv()

        @pl.when(has_high)
        def _():
            down(root).wait_recv()

        stage[0] = low[root]
        stage[1] = own[root]
        stage[2] = high[root]
        for slot in range(slots):
            source = stage[deltas_ref[slot] + 1]
            mixed[:, slot * width:(slot + 1) * width] = jnp.dot(
                left[slot], source, preferred_element_type=jnp.float32
            ).astype(mixed.dtype)
        total = jnp.dot(mixed[...], right_t[...], preferred_element_type=jnp.float32)
        now = lax.rem(root, 2)

        @pl.when(root >= 2)
        def _():
            out_copy(root - 2, now).wait()

        result[now] = total.astype(result.dtype)
        out_copy(root, now).start()

        if rows:
            @pl.when(root < forwards)
            def _():
                aside(root, root, 0, me).wait_recv()

                @pl.when(up_relay)
                def _():
                    forward(root, low, low_sem).start()

                @pl.when(down_relay)
                def _():
                    forward(root, high, high_sem).start()

    for root in (roots - 2, roots - 1):
        out_copy(root, root % 2).wait()

    @pl.loop(0, roots)
    def _(root):
        @pl.when(has_high)
        def _():
            up(root).wait_send()

        @pl.when(has_low)
        def _():
            down(root).wait_send()

        if rows:
            @pl.when(root < forwards)
            def _():
                forward(root, low, low_sem).wait_send()


def on_device(sectors, wave, left_ops, right_ops, deltas, counts):
    wave = wave[0]
    roots, width = wave.shape[0], wave.shape[1]
    slots = left_ops.shape[0]
    block = (roots, width, width)
    bf16 = wave.dtype
    flops = 4 * roots * slots * width**3
    sigma = pl.pallas_call(
        functools.partial(kernel, sectors),
        out_shape=jax.ShapeDtypeStruct(block, bf16),
        in_specs=[pl.BlockSpec(memory_space=pltpu.SMEM)] * 2 + [pl.BlockSpec(memory_space=pl.ANY)] * 3,
        out_specs=pl.BlockSpec(memory_space=pl.ANY),
        scratch_shapes=[
            pltpu.VMEM(block, bf16),
            pltpu.VMEM(block, bf16),
            pltpu.VMEM(block, bf16),
            pltpu.VMEM(block, bf16),
            pltpu.VMEM((slots, width, width), bf16),
            pltpu.VMEM((slots, width, width), bf16),
            pltpu.VMEM((slots * width, width), bf16),
            pltpu.VMEM((3, width, width), bf16),
            pltpu.VMEM((width, slots * width), bf16),
            pltpu.VMEM((2, width, width), bf16),
            pltpu.SemaphoreType.DMA((2, roots)),
            pltpu.SemaphoreType.DMA((roots,)),
            pltpu.SemaphoreType.DMA((roots,)),
            pltpu.SemaphoreType.DMA((roots,)),
            pltpu.SemaphoreType.DMA((roots,)),
            pltpu.SemaphoreType.DMA,
            pltpu.SemaphoreType.DMA((2,)),
            pltpu.SemaphoreType.DMA((2,)),
        ],
        compiler_params=pltpu.CompilerParams(
            collective_id=0, has_side_effects=True, vmem_limit_bytes=60 * 2**20
        ),
        cost_estimate=pl.CostEstimate(flops=flops, bytes_accessed=7 * 2**20, transcendentals=0),
    )(counts, deltas, wave, left_ops, right_ops)
    return sigma[None]


def solution(mesh):
    return jax.shard_map(
        functools.partial(on_device, mesh.shape["sector"]),
        mesh=mesh,
        in_specs=(
            P(("group", "sector"), None, None, None),
            P(("group", "sector"), None, None),
            P(("group", "sector"), None, None),
            P(("group", "sector")),
            P(("group", "sector")),
        ),
        out_specs=P(("group", "sector"), None, None, None),
        check_vma=False,
    )
```

```python
import functools

import jax
import jax.numpy as jnp
from jax import lax
from jax.experimental import pallas as pl
from jax.experimental.pallas import tpu as pltpu
from jax.sharding import PartitionSpec as P

MESH = pl.DeviceIdType.MESH


def kernel(
    sectors, counts_ref, deltas_ref, wave_ref, left_ref, right_ref, out_ref,
    own, low, high, passing, left, right, right_t, stage, mixed, offsets,
    send_sem, low_sem, high_sem, passing_sem, forward_sem, own_sem, op_sem,
):
    roots, width = own.shape[0], own.shape[1]
    slots = left.shape[0]
    me = lax.axis_index("sector")
    has_low, has_high = me > 0, me < sectors - 1

    rows = sectors // 4 if sectors == 16 else 0
    row, place = lax.div(me, 4), lax.rem(me, 4)
    above, below = row < rows - 1, jnp.logical_and(row > 0, row < rows)
    up_source = jnp.logical_and(place == 3, above)
    up_relay = jnp.logical_and(place == 1, above)
    down_source = jnp.logical_and(place == 0, below)
    down_relay = jnp.logical_and(place == 2, below)
    up_share = lax.div(roots * (rows - 1 - row), max(rows, 1))
    down_share = lax.div(roots * row, max(rows, 1))
    up_detour = jnp.where(up_source, up_share, 0)
    down_detour = jnp.where(down_source, down_share, 0)
    forwards = jnp.where(up_relay, up_share, jnp.where(down_relay, down_share, 0))
    ahead = jnp.where(up_relay, me + 3, jnp.where(down_relay, me - 3, me))

    partners = [(has_low, me - 1), (has_high, me + 1)]
    if rows:
        partners += [
            (up_source, me - 2), (up_source, me + 3),
            (down_source, me + 2), (down_source, me - 3),
            (up_relay, me + 2), (up_relay, me + 3),
            (down_relay, me - 2), (down_relay, me - 3),
        ]
    barrier = pltpu.get_barrier_semaphore()
    for present, partner in partners:
        @pl.when(present)
        def _(partner=partner):
            pl.semaphore_signal(barrier, inc=1, device_id={"sector": partner}, device_id_type=MESH)

    left_copy = pltpu.make_async_copy(left_ref, left, op_sem.at[0])
    right_copy = pltpu.make_async_copy(right_ref, right, op_sem.at[1])
    own_copy = pltpu.make_async_copy(wave_ref, own, own_sem)
    offsets_copy = pltpu.make_async_copy(deltas_ref, offsets, op_sem.at[2])
    offsets_copy.start()
    left_copy.start()
    right_copy.start()
    own_copy.start()
    pl.semaphore_wait(barrier, sum(present.astype(jnp.int32) for present, _ in partners))

    def up(root):
        return pltpu.make_async_remote_copy(
            src_ref=wave_ref.at[root], dst_ref=low.at[root],
            send_sem=send_sem.at[0, root], recv_sem=low_sem.at[root],
            device_id={"sector": me + 1}, device_id_type=MESH,
        )

    def down(root):
        return pltpu.make_async_remote_copy(
            src_ref=wave_ref.at[root], dst_ref=high.at[root],
            send_sem=send_sem.at[1, root], recv_sem=high_sem.at[root],
            device_id={"sector": me - 1}, device_id_type=MESH,
        )

    def aside(root, step, way, corner):
        return pltpu.make_async_remote_copy(
            src_ref=wave_ref.at[root], dst_ref=passing.at[step],
            send_sem=send_sem.at[way, root], recv_sem=passing_sem.at[step],
            device_id={"sector": corner}, device_id_type=MESH,
        )

    def forward(step, target, target_sem):
        root = roots - forwards + step
        return pltpu.make_async_remote_copy(
            src_ref=passing.at[step], dst_ref=target.at[root],
            send_sem=forward_sem.at[step], recv_sem=target_sem.at[root],
            device_id={"sector": ahead}, device_id_type=MESH,
        )

    @pl.loop(0, roots)
    def _(step):
        @pl.when(jnp.logical_and(has_high, step < roots - up_detour))
        def _():
            up(step).start()

        @pl.when(jnp.logical_and(has_low, step < roots - down_detour))
        def _():
            down(step).start()

        if rows:
            @pl.when(step < up_detour)
            def _():
                aside(roots - up_detour + step, step, 0, me - 2).start()

            @pl.when(step < down_detour)
            def _():
                aside(roots - down_detour + step, step, 1, me + 2).start()

    @pl.when(jnp.logical_not(has_low))
    def _():
        low[...] = jnp.zeros_like(low)

    @pl.when(jnp.logical_not(has_high))
    def _():
        high[...] = jnp.zeros_like(high)

    left_copy.wait()
    right_copy.wait()
    offsets_copy.wait()
    count = counts_ref[0]

    @pl.loop(0, slots)
    def _(slot):
        live = jnp.where(slot < count, 1.0, 0.0).astype(jnp.float32)
        left[slot] = (left[slot].astype(jnp.float32) * live).astype(left.dtype)
        right_t[pl.ds(pl.multiple_of(slot * width, width), width), :] = right[slot].T

    own_copy.wait()

    @pl.loop(0, roots)
    def _(root):
        @pl.when(has_low)
        def _():
            up(root).wait_recv()

        @pl.when(has_high)
        def _():
            down(root).wait_recv()

        stage[0] = low[root]
        stage[1] = own[root]
        stage[2] = high[root]
        for slot in range(slots):
            source = stage[offsets[slot] + 1]
            mixed[:, slot * width:(slot + 1) * width] = jnp.dot(
                left[slot], source, preferred_element_type=jnp.float32
            ).astype(mixed.dtype)
        total = jnp.dot(mixed[...], right_t[...], preferred_element_type=jnp.float32)
        out_ref[root] = total.astype(out_ref.dtype)

        if rows:
            @pl.when(root < forwards)
            def _():
                aside(root, root, 0, me).wait_recv()

                @pl.when(up_relay)
                def _():
                    forward(root, low, low_sem).start()

                @pl.when(down_relay)
                def _():
                    forward(root, high, high_sem).start()

    @pl.loop(0, roots)
    def _(root):
        @pl.when(has_high)
        def _():
            up(root).wait_send()

        @pl.when(has_low)
        def _():
            down(root).wait_send()

        if rows:
            @pl.when(root < forwards)
            def _():
                forward(root, low, low_sem).wait_send()


def on_device(sectors, wave, left_ops, right_ops, deltas, counts):
    wave = wave[0]
    wave, left_ops, right_ops, deltas = (
        pltpu.with_memory_space_constraint(x, pltpu.HBM)
        for x in (wave, left_ops, right_ops, deltas)
    )
    roots, width = wave.shape[0], wave.shape[1]
    slots = left_ops.shape[0]
    block = (roots, width, width)
    bf16 = wave.dtype
    flops = 4 * roots * slots * width**3
    sigma = pl.pallas_call(
        functools.partial(kernel, sectors),
        out_shape=pltpu.VMEM(block, bf16),
        in_specs=[pl.BlockSpec(memory_space=pltpu.SMEM)] + [pl.BlockSpec(memory_space=pltpu.HBM)] * 4,
        out_specs=pl.BlockSpec(memory_space=pltpu.VMEM),
        scratch_shapes=[
            pltpu.VMEM(block, bf16),
            pltpu.VMEM(block, bf16),
            pltpu.VMEM(block, bf16),
            pltpu.VMEM(block, bf16),
            pltpu.VMEM((slots, width, width), bf16),
            pltpu.VMEM((slots, width, width), bf16),
            pltpu.VMEM((slots * width, width), bf16),
            pltpu.VMEM((3, width, width), bf16),
            pltpu.VMEM((width, slots * width), bf16),
            pltpu.SMEM(deltas.shape, deltas.dtype),
            pltpu.SemaphoreType.DMA((2, roots)),
            pltpu.SemaphoreType.DMA((roots,)),
            pltpu.SemaphoreType.DMA((roots,)),
            pltpu.SemaphoreType.DMA((roots,)),
            pltpu.SemaphoreType.DMA((roots,)),
            pltpu.SemaphoreType.DMA,
            pltpu.SemaphoreType.DMA((3,)),
        ],
        compiler_params=pltpu.CompilerParams(
            collective_id=0, has_side_effects=True, vmem_limit_bytes=48 * 2**20
        ),
        cost_estimate=pl.CostEstimate(flops=flops, bytes_accessed=7 * 2**20, transcendentals=0),
    )(counts, deltas, wave, left_ops, right_ops)
    return sigma[None]


def solution(mesh):
    return jax.shard_map(
        functools.partial(on_device, mesh.shape["sector"]),
        mesh=mesh,
        in_specs=(
            P(("group", "sector"), None, None, None),
            P(("group", "sector"), None, None),
            P(("group", "sector"), None, None),
            P(("group", "sector")),
            P(("group", "sector")),
        ),
        out_specs=P(("group", "sector"), None, None, None),
        check_vma=False,
    )
```

```python
import functools

import jax
import jax.numpy as jnp
from jax import lax
from jax.experimental import pallas as pl
from jax.experimental.pallas import tpu as pltpu
from jax.sharding import PartitionSpec as P

MESH = pl.DeviceIdType.MESH


def apply_root(stage, offsets, left, right_t, mixed):
    slots, width = left.shape[0], left.shape[1]
    for slot in range(slots):
        source = stage[offsets[slot] + 1]
        mixed[:, slot * width:(slot + 1) * width] = jnp.dot(
            left[slot], source, preferred_element_type=jnp.float32
        ).astype(mixed.dtype)
    return jnp.dot(mixed[...], right_t[...], preferred_element_type=jnp.float32)


def finish(offsets, stage, left, right_t, done_ref, out_ref, mixed, result, done_sem, last_sem):
    last = out_ref.shape[0] - 1
    done_copy = pltpu.make_async_copy(
        done_ref.at[pl.ds(0, last)], out_ref.at[pl.ds(0, last)], done_sem
    )
    done_copy.start()
    result[...] = apply_root(stage, offsets, left, right_t, mixed).astype(result.dtype)
    last_copy = pltpu.make_async_copy(result, out_ref.at[last], last_sem)
    last_copy.start()
    done_copy.wait()
    last_copy.wait()


def kernel(
    sectors, counts_ref, deltas_ref, wave_ref, left_ref, right_ref,
    out_ref, left, right_t, stage, offsets,
    own, low, high, passing, right, mixed,
    send_sem, low_sem, high_sem, passing_sem, forward_sem, own_sem, op_sem,
):
    roots, width = own.shape[0], own.shape[1]
    slots = left.shape[0]
    me = lax.axis_index("sector")
    has_low, has_high = me > 0, me < sectors - 1

    rows = sectors // 4 if sectors == 16 else 0
    row, place = lax.div(me, 4), lax.rem(me, 4)
    above, below = row < rows - 1, jnp.logical_and(row > 0, row < rows)
    up_source = jnp.logical_and(place == 3, above)
    up_relay = jnp.logical_and(place == 1, above)
    down_source = jnp.logical_and(place == 0, below)
    down_relay = jnp.logical_and(place == 2, below)
    up_share = lax.div(roots * (rows - 1 - row), max(rows, 1))
    down_share = lax.div(roots * row, max(rows, 1))
    up_detour = jnp.where(up_source, up_share, 0)
    down_detour = jnp.where(down_source, down_share, 0)
    forwards = jnp.where(up_relay, up_share, jnp.where(down_relay, down_share, 0))
    ahead = jnp.where(up_relay, me + 3, jnp.where(down_relay, me - 3, me))

    partners = [(has_low, me - 1), (has_high, me + 1)]
    if rows:
        partners += [
            (up_source, me - 2), (up_source, me + 3),
            (down_source, me + 2), (down_source, me - 3),
            (up_relay, me + 2), (up_relay, me + 3),
            (down_relay, me - 2), (down_relay, me - 3),
        ]
    barrier = pltpu.get_barrier_semaphore()
    for present, partner in partners:
        @pl.when(present)
        def _(partner=partner):
            pl.semaphore_signal(barrier, inc=1, device_id={"sector": partner}, device_id_type=MESH)

    left_copy = pltpu.make_async_copy(left_ref, left, op_sem.at[0])
    right_copy = pltpu.make_async_copy(right_ref, right, op_sem.at[1])
    own_copy = pltpu.make_async_copy(wave_ref, own, own_sem)
    offsets_copy = pltpu.make_async_copy(deltas_ref, offsets, op_sem.at[2])
    offsets_copy.start()
    left_copy.start()
    right_copy.start()
    own_copy.start()
    pl.semaphore_wait(barrier, sum(present.astype(jnp.int32) for present, _ in partners))

    def up(root):
        return pltpu.make_async_remote_copy(
            src_ref=wave_ref.at[root], dst_ref=low.at[root],
            send_sem=send_sem.at[0, root], recv_sem=low_sem.at[root],
            device_id={"sector": me + 1}, device_id_type=MESH,
        )

    def down(root):
        return pltpu.make_async_remote_copy(
            src_ref=wave_ref.at[root], dst_ref=high.at[root],
            send_sem=send_sem.at[1, root], recv_sem=high_sem.at[root],
            device_id={"sector": me - 1}, device_id_type=MESH,
        )

    def aside(root, step, way, corner):
        return pltpu.make_async_remote_copy(
            src_ref=wave_ref.at[root], dst_ref=passing.at[step],
            send_sem=send_sem.at[way, root], recv_sem=passing_sem.at[step],
            device_id={"sector": corner}, device_id_type=MESH,
        )

    def forward(step, target, target_sem):
        root = roots - forwards + step
        return pltpu.make_async_remote_copy(
            src_ref=passing.at[step], dst_ref=target.at[root],
            send_sem=forward_sem.at[step], recv_sem=target_sem.at[root],
            device_id={"sector": ahead}, device_id_type=MESH,
        )

    @pl.loop(0, roots)
    def _(step):
        @pl.when(jnp.logical_and(has_high, step < roots - up_detour))
        def _():
            up(step).start()

        @pl.when(jnp.logical_and(has_low, step < roots - down_detour))
        def _():
            down(step).start()

        if rows:
            @pl.when(step < up_detour)
            def _():
                aside(roots - up_detour + step, step, 0, me - 2).start()

            @pl.when(step < down_detour)
            def _():
                aside(roots - down_detour + step, step, 1, me + 2).start()

    @pl.when(jnp.logical_not(has_low))
    def _():
        low[...] = jnp.zeros_like(low)

    @pl.when(jnp.logical_not(has_high))
    def _():
        high[...] = jnp.zeros_like(high)

    left_copy.wait()
    right_copy.wait()
    offsets_copy.wait()
    count = counts_ref[0]

    @pl.loop(0, slots)
    def _(slot):
        live = jnp.where(slot < count, 1.0, 0.0).astype(jnp.float32)
        left[slot] = (left[slot].astype(jnp.float32) * live).astype(left.dtype)
        right_t[pl.ds(pl.multiple_of(slot * width, width), width), :] = right[slot].T

    own_copy.wait()

    def gather(root):
        @pl.when(has_low)
        def _():
            up(root).wait_recv()

        @pl.when(has_high)
        def _():
            down(root).wait_recv()

        stage[0] = low[root]
        stage[1] = own[root]
        stage[2] = high[root]

    def settle(root):
        @pl.when(has_high)
        def _():
            up(root).wait_send()

        @pl.when(has_low)
        def _():
            down(root).wait_send()

        if rows:
            @pl.when(root < forwards)
            def _():
                forward(root, low, low_sem).wait_send()

    @pl.loop(0, roots - 1)
    def _(root):
        gather(root)
        total = apply_root(stage, offsets, left, right_t, mixed)
        out_ref[root] = total.astype(out_ref.dtype)

        if rows:
            @pl.when(root < forwards)
            def _():
                aside(root, root, 0, me).wait_recv()

                @pl.when(up_relay)
                def _():
                    forward(root, low, low_sem).start()

                @pl.when(down_relay)
                def _():
                    forward(root, high, high_sem).start()

        @pl.when(root >= 4)
        def _():
            settle(root - 4)

    gather(roots - 1)

    @pl.loop(roots - 5, roots)
    def _(root):
        settle(root)


def on_device(sectors, wave, left_ops, right_ops, deltas, counts):
    wave = wave[0]
    wave, left_ops, right_ops, deltas = (
        pltpu.with_memory_space_constraint(x, pltpu.HBM)
        for x in (wave, left_ops, right_ops, deltas)
    )
    roots, width = wave.shape[0], wave.shape[1]
    slots = left_ops.shape[0]
    block = (roots, width, width)
    bf16 = wave.dtype
    flops = 4 * roots * slots * width**3
    operand = (slots, width, width)
    operand_cat = (slots * width, width)
    held = pl.BlockSpec(memory_space=pltpu.VMEM)
    scalars = pl.BlockSpec(memory_space=pltpu.SMEM)
    done, left, right_t, stage, offsets = pl.pallas_call(
        functools.partial(kernel, sectors),
        out_shape=(
            pltpu.VMEM(block, bf16),
            pltpu.VMEM(operand, bf16),
            pltpu.VMEM(operand_cat, bf16),
            pltpu.VMEM((3, width, width), bf16),
            pltpu.SMEM(deltas.shape, deltas.dtype),
        ),
        in_specs=[scalars] + [pl.BlockSpec(memory_space=pltpu.HBM)] * 4,
        out_specs=(held, held, held, held, scalars),
        scratch_shapes=[
            pltpu.VMEM(block, bf16),
            pltpu.VMEM(block, bf16),
            pltpu.VMEM(block, bf16),
            pltpu.VMEM(block, bf16),
            pltpu.VMEM(operand, bf16),
            pltpu.VMEM((width, slots * width), bf16),
            pltpu.SemaphoreType.DMA((2, roots)),
            pltpu.SemaphoreType.DMA((roots,)),
            pltpu.SemaphoreType.DMA((roots,)),
            pltpu.SemaphoreType.DMA((roots,)),
            pltpu.SemaphoreType.DMA((roots,)),
            pltpu.SemaphoreType.DMA,
            pltpu.SemaphoreType.DMA((3,)),
        ],
        compiler_params=pltpu.CompilerParams(
            collective_id=0, has_side_effects=True, vmem_limit_bytes=48 * 2**20
        ),
        cost_estimate=pl.CostEstimate(flops=flops, bytes_accessed=7 * 2**20, transcendentals=0),
    )(counts, deltas, wave, left_ops, right_ops)
    sigma = pl.pallas_call(
        finish,
        out_shape=jax.ShapeDtypeStruct(block, bf16),
        in_specs=[scalars] + [held] * 4,
        out_specs=pl.BlockSpec(memory_space=pl.ANY),
        scratch_shapes=[
            pltpu.VMEM((width, slots * width), bf16),
            pltpu.VMEM((width, width), bf16),
            pltpu.SemaphoreType.DMA,
            pltpu.SemaphoreType.DMA,
        ],
        compiler_params=pltpu.CompilerParams(vmem_limit_bytes=48 * 2**20),
        cost_estimate=pl.CostEstimate(
            flops=flops // roots, bytes_accessed=2 * 2**20, transcendentals=0
        ),
    )(offsets, stage, left, right_t, done)
    return sigma[None]


def solution(mesh):
    return jax.shard_map(
        functools.partial(on_device, mesh.shape["sector"]),
        mesh=mesh,
        in_specs=(
            P(("group", "sector"), None, None, None),
            P(("group", "sector"), None, None),
            P(("group", "sector"), None, None),
            P(("group", "sector")),
            P(("group", "sector")),
        ),
        out_specs=P(("group", "sector"), None, None, None),
        check_vma=False,
    )
```

```python
import functools

import jax
import jax.numpy as jnp
from jax import lax
from jax.experimental import pallas as pl
from jax.experimental.pallas import tpu as pltpu
from jax.sharding import PartitionSpec as P

MESH = pl.DeviceIdType.MESH


def apply_root(stage, offsets, left, right_t, mixed):
    slots, width = left.shape[0], left.shape[1]
    group = 3 if slots % 3 == 0 else 1
    total = None
    for first in range(0, slots, group):
        for slot in range(first, first + group):
            source = stage[offsets[slot] + 1]
            mixed[:, slot * width:(slot + 1) * width] = jnp.dot(
                left[slot], source, preferred_element_type=jnp.float32
            ).astype(mixed.dtype)
        span = slice(first * width, (first + group) * width)
        part = jnp.dot(mixed[:, span], right_t[span, :], preferred_element_type=jnp.float32)
        total = part if total is None else total + part
    return total


def finish(offsets, stage, left, right_t, done_ref, out_ref, mixed, result, done_sem, last_sem):
    last = out_ref.shape[0] - 1
    done_copy = pltpu.make_async_copy(
        done_ref.at[pl.ds(0, last)], out_ref.at[pl.ds(0, last)], done_sem
    )
    done_copy.start()
    result[...] = apply_root(stage, offsets, left, right_t, mixed).astype(result.dtype)
    last_copy = pltpu.make_async_copy(result, out_ref.at[last], last_sem)
    last_copy.start()
    done_copy.wait()
    last_copy.wait()


def kernel(
    sectors, counts_ref, deltas_ref, wave_ref, left_ref, right_ref,
    out_ref, left, right_t, stage, offsets,
    own, low, high, passing, right, mixed,
    send_sem, low_sem, high_sem, passing_sem, forward_sem, own_sem, op_sem,
):
    roots, width = own.shape[0], own.shape[1]
    slots = left.shape[0]
    me = lax.axis_index("sector")
    has_low, has_high = me > 0, me < sectors - 1

    rows = sectors // 4 if sectors == 16 else 0
    row, place = lax.div(me, 4), lax.rem(me, 4)
    above, below = row < rows - 1, jnp.logical_and(row > 0, row < rows)
    up_source = jnp.logical_and(place == 3, above)
    up_relay = jnp.logical_and(place == 1, above)
    down_source = jnp.logical_and(place == 0, below)
    down_relay = jnp.logical_and(place == 2, below)
    up_share = lax.div(roots * (rows - 1 - row), max(rows, 1))
    down_share = lax.div(roots * row, max(rows, 1))
    up_detour = jnp.where(up_source, up_share, 0)
    down_detour = jnp.where(down_source, down_share, 0)
    forwards = jnp.where(up_relay, up_share, jnp.where(down_relay, down_share, 0))
    ahead = jnp.where(up_relay, me + 3, jnp.where(down_relay, me - 3, me))

    partners = [(has_low, me - 1), (has_high, me + 1)]
    if rows:
        partners += [
            (up_source, me - 2), (up_source, me + 3),
            (down_source, me + 2), (down_source, me - 3),
            (up_relay, me + 2), (up_relay, me + 3),
            (down_relay, me - 2), (down_relay, me - 3),
        ]
    barrier = pltpu.get_barrier_semaphore()
    for present, partner in partners:
        @pl.when(present)
        def _(partner=partner):
            pl.semaphore_signal(barrier, inc=1, device_id={"sector": partner}, device_id_type=MESH)

    left_copy = pltpu.make_async_copy(left_ref, left, op_sem.at[0])
    right_copy = pltpu.make_async_copy(right_ref, right, op_sem.at[1])
    own_copy = pltpu.make_async_copy(wave_ref, own, own_sem)
    offsets_copy = pltpu.make_async_copy(deltas_ref, offsets, op_sem.at[2])
    offsets_copy.start()
    left_copy.start()
    right_copy.start()
    own_copy.start()
    pl.semaphore_wait(barrier, sum(present.astype(jnp.int32) for present, _ in partners))

    def up(root):
        return pltpu.make_async_remote_copy(
            src_ref=wave_ref.at[root], dst_ref=low.at[root],
            send_sem=send_sem.at[0, root], recv_sem=low_sem.at[root],
            device_id={"sector": me + 1}, device_id_type=MESH,
        )

    def down(root):
        return pltpu.make_async_remote_copy(
            src_ref=wave_ref.at[root], dst_ref=high.at[root],
            send_sem=send_sem.at[1, root], recv_sem=high_sem.at[root],
            device_id={"sector": me - 1}, device_id_type=MESH,
        )

    def aside(root, step, way, corner):
        return pltpu.make_async_remote_copy(
            src_ref=wave_ref.at[root], dst_ref=passing.at[step],
            send_sem=send_sem.at[way, root], recv_sem=passing_sem.at[step],
            device_id={"sector": corner}, device_id_type=MESH,
        )

    def forward(step, target, target_sem):
        root = roots - forwards + step
        return pltpu.make_async_remote_copy(
            src_ref=passing.at[step], dst_ref=target.at[root],
            send_sem=forward_sem.at[step], recv_sem=target_sem.at[root],
            device_id={"sector": ahead}, device_id_type=MESH,
        )

    @pl.loop(0, roots)
    def _(step):
        @pl.when(jnp.logical_and(has_high, step < roots - up_detour))
        def _():
            up(step).start()

        @pl.when(jnp.logical_and(has_low, step < roots - down_detour))
        def _():
            down(step).start()

        if rows:
            @pl.when(step < up_detour)
            def _():
                aside(roots - up_detour + step, step, 0, me - 2).start()

            @pl.when(step < down_detour)
            def _():
                aside(roots - down_detour + step, step, 1, me + 2).start()

    @pl.when(jnp.logical_not(has_low))
    def _():
        low[...] = jnp.zeros_like(low)

    @pl.when(jnp.logical_not(has_high))
    def _():
        high[...] = jnp.zeros_like(high)

    left_copy.wait()
    right_copy.wait()
    offsets_copy.wait()
    count = counts_ref[0]

    @pl.loop(0, slots)
    def _(slot):
        live = jnp.where(slot < count, 1.0, 0.0).astype(jnp.float32)
        left[slot] = (left[slot].astype(jnp.float32) * live).astype(left.dtype)
        right_t[pl.ds(pl.multiple_of(slot * width, width), width), :] = right[slot].T

    own_copy.wait()

    def gather(root):
        @pl.when(has_low)
        def _():
            up(root).wait_recv()

        @pl.when(has_high)
        def _():
            down(root).wait_recv()

        stage[0] = low[root]
        stage[1] = own[root]
        stage[2] = high[root]

    def settle(root):
        @pl.when(has_high)
        def _():
            up(root).wait_send()

        @pl.when(has_low)
        def _():
            down(root).wait_send()

        if rows:
            @pl.when(root < forwards)
            def _():
                forward(root, low, low_sem).wait_send()

    @pl.loop(0, roots - 1)
    def _(root):
        gather(root)
        total = apply_root(stage, offsets, left, right_t, mixed)
        out_ref[root] = total.astype(out_ref.dtype)

        if rows:
            @pl.when(root < forwards)
            def _():
                aside(root, root, 0, me).wait_recv()

                @pl.when(up_relay)
                def _():
                    forward(root, low, low_sem).start()

                @pl.when(down_relay)
                def _():
                    forward(root, high, high_sem).start()

        @pl.when(root >= 4)
        def _():
            settle(root - 4)

    gather(roots - 1)

    @pl.loop(roots - 5, roots)
    def _(root):
        settle(root)


def on_device(sectors, wave, left_ops, right_ops, deltas, counts):
    wave = wave[0]
    wave, left_ops, right_ops, deltas = (
        pltpu.with_memory_space_constraint(x, pltpu.HBM)
        for x in (wave, left_ops, right_ops, deltas)
    )
    roots, width = wave.shape[0], wave.shape[1]
    slots = left_ops.shape[0]
    block = (roots, width, width)
    bf16 = wave.dtype
    flops = 4 * roots * slots * width**3
    operand = (slots, width, width)
    operand_cat = (slots * width, width)
    held = pl.BlockSpec(memory_space=pltpu.VMEM)
    scalars = pl.BlockSpec(memory_space=pltpu.SMEM)
    done, left, right_t, stage, offsets = pl.pallas_call(
        functools.partial(kernel, sectors),
        out_shape=(
            pltpu.VMEM(block, bf16),
            pltpu.VMEM(operand, bf16),
            pltpu.VMEM(operand_cat, bf16),
            pltpu.VMEM((3, width, width), bf16),
            pltpu.SMEM(deltas.shape, deltas.dtype),
        ),
        in_specs=[scalars] + [pl.BlockSpec(memory_space=pltpu.HBM)] * 4,
        out_specs=(held, held, held, held, scalars),
        scratch_shapes=[
            pltpu.VMEM(block, bf16),
            pltpu.VMEM(block, bf16),
            pltpu.VMEM(block, bf16),
            pltpu.VMEM(block, bf16),
            pltpu.VMEM(operand, bf16),
            pltpu.VMEM((width, slots * width), bf16),
            pltpu.SemaphoreType.DMA((2, roots)),
            pltpu.SemaphoreType.DMA((roots,)),
            pltpu.SemaphoreType.DMA((roots,)),
            pltpu.SemaphoreType.DMA((roots,)),
            pltpu.SemaphoreType.DMA((roots,)),
            pltpu.SemaphoreType.DMA,
            pltpu.SemaphoreType.DMA((3,)),
        ],
        compiler_params=pltpu.CompilerParams(
            collective_id=0, has_side_effects=True, vmem_limit_bytes=48 * 2**20
        ),
        cost_estimate=pl.CostEstimate(flops=flops, bytes_accessed=7 * 2**20, transcendentals=0),
    )(counts, deltas, wave, left_ops, right_ops)
    sigma = pl.pallas_call(
        finish,
        out_shape=jax.ShapeDtypeStruct(block, bf16),
        in_specs=[scalars] + [held] * 4,
        out_specs=pl.BlockSpec(memory_space=pl.ANY),
        scratch_shapes=[
            pltpu.VMEM((width, slots * width), bf16),
            pltpu.VMEM((width, width), bf16),
            pltpu.SemaphoreType.DMA,
            pltpu.SemaphoreType.DMA,
        ],
        compiler_params=pltpu.CompilerParams(vmem_limit_bytes=48 * 2**20),
        cost_estimate=pl.CostEstimate(
            flops=flops // roots, bytes_accessed=2 * 2**20, transcendentals=0
        ),
    )(offsets, stage, left, right_t, done)
    return sigma[None]


def solution(mesh):
    return jax.shard_map(
        functools.partial(on_device, mesh.shape["sector"]),
        mesh=mesh,
        in_specs=(
            P(("group", "sector"), None, None, None),
            P(("group", "sector"), None, None),
            P(("group", "sector"), None, None),
            P(("group", "sector")),
            P(("group", "sector")),
        ),
        out_specs=P(("group", "sector"), None, None, None),
        check_vma=False,
    )
```

```python
import functools

import jax
import jax.numpy as jnp
from jax import lax
from jax.experimental import pallas as pl
from jax.experimental.pallas import tpu as pltpu
from jax.sharding import PartitionSpec as P

MESH = pl.DeviceIdType.MESH


def apply_root(stage, offsets, left, right_t, mixed):
    slots, width = left.shape[0], left.shape[1]
    for slot in range(slots):
        source = stage[offsets[slot] + 1]
        mixed[:, slot * width:(slot + 1) * width] = jnp.dot(
            left[slot], source, preferred_element_type=jnp.float32
        ).astype(mixed.dtype)
    return jnp.dot(mixed[...], right_t[...], preferred_element_type=jnp.float32)


def finish(offsets, stage, left, right_t, done_ref, out_ref, mixed, result, done_sem, last_sem):
    last = out_ref.shape[0] - 1
    done_copy = pltpu.make_async_copy(
        done_ref.at[pl.ds(0, last)], out_ref.at[pl.ds(0, last)], done_sem
    )
    done_copy.start()
    result[...] = apply_root(stage, offsets, left, right_t, mixed).astype(result.dtype)
    last_copy = pltpu.make_async_copy(result, out_ref.at[last], last_sem)
    last_copy.start()
    done_copy.wait()
    last_copy.wait()


def kernel(
    sectors, counts_ref, deltas_ref, wave_ref, left_ref, right_ref,
    out_ref, left, right_t, stage, offsets,
    own, low, high, passing, right, mixed,
    send_sem, low_sem, high_sem, passing_sem, forward_sem, own_sem, op_sem,
):
    roots, width = own.shape[0], own.shape[1]
    slots = left.shape[0]
    me = lax.axis_index("sector")
    has_low, has_high = me > 0, me < sectors - 1

    rows = sectors // 4 if sectors == 16 else 0
    row, place = lax.div(me, 4), lax.rem(me, 4)
    above, below = row < rows - 1, jnp.logical_and(row > 0, row < rows)
    up_source = jnp.logical_and(place == 3, above)
    up_relay = jnp.logical_and(place == 1, above)
    down_source = jnp.logical_and(place == 0, below)
    down_relay = jnp.logical_and(place == 2, below)
    up_share = lax.div(roots * (rows - 1 - row), max(rows, 1))
    down_share = lax.div(roots * row, max(rows, 1))
    up_detour = jnp.where(up_source, up_share, 0)
    down_detour = jnp.where(down_source, down_share, 0)
    forwards = jnp.where(up_relay, up_share, jnp.where(down_relay, down_share, 0))
    ahead = jnp.where(up_relay, me + 3, jnp.where(down_relay, me - 3, me))

    partners = [(has_low, me - 1), (has_high, me + 1)]
    if rows:
        partners += [
            (up_source, me - 2), (up_source, me + 3),
            (down_source, me + 2), (down_source, me - 3),
            (up_relay, me + 2), (up_relay, me + 3),
            (down_relay, me - 2), (down_relay, me - 3),
        ]
    barrier = pltpu.get_barrier_semaphore()
    for present, partner in partners:
        @pl.when(present)
        def _(partner=partner):
            pl.semaphore_signal(barrier, inc=1, device_id={"sector": partner}, device_id_type=MESH)

    left_copy = pltpu.make_async_copy(left_ref, left, op_sem.at[0])
    right_copy = pltpu.make_async_copy(right_ref, right, op_sem.at[1])
    own_copy = pltpu.make_async_copy(wave_ref, own, own_sem)
    offsets_copy = pltpu.make_async_copy(deltas_ref, offsets, op_sem.at[2])
    pl.semaphore_wait(barrier, sum(present.astype(jnp.int32) for present, _ in partners))

    def up(root):
        return pltpu.make_async_remote_copy(
            src_ref=wave_ref.at[root], dst_ref=low.at[root],
            send_sem=send_sem.at[0, root], recv_sem=low_sem.at[root],
            device_id={"sector": me + 1}, device_id_type=MESH,
        )

    def down(root):
        return pltpu.make_async_remote_copy(
            src_ref=wave_ref.at[root], dst_ref=high.at[root],
            send_sem=send_sem.at[1, root], recv_sem=high_sem.at[root],
            device_id={"sector": me - 1}, device_id_type=MESH,
        )

    def aside(root, step, way, corner):
        return pltpu.make_async_remote_copy(
            src_ref=wave_ref.at[root], dst_ref=passing.at[step],
            send_sem=send_sem.at[way, root], recv_sem=passing_sem.at[step],
            device_id={"sector": corner}, device_id_type=MESH,
        )

    def forward(step, target, target_sem):
        root = roots - forwards + step
        return pltpu.make_async_remote_copy(
            src_ref=passing.at[step], dst_ref=target.at[root],
            send_sem=forward_sem.at[step], recv_sem=target_sem.at[root],
            device_id={"sector": ahead}, device_id_type=MESH,
        )

    def send(step):
        @pl.when(jnp.logical_and(has_high, step < roots - up_detour))
        def _():
            up(step).start()

        @pl.when(jnp.logical_and(has_low, step < roots - down_detour))
        def _():
            down(step).start()

        if rows:
            @pl.when(step < up_detour)
            def _():
                aside(roots - up_detour + step, step, 0, me - 2).start()

            @pl.when(step < down_detour)
            def _():
                aside(roots - down_detour + step, step, 1, me + 2).start()

    lead = 2

    @pl.loop(0, lead)
    def _(step):
        send(step)

    offsets_copy.start()
    left_copy.start()
    right_copy.start()
    own_copy.start()

    @pl.loop(lead, roots)
    def _(step):
        send(step)

    @pl.when(jnp.logical_not(has_low))
    def _():
        low[...] = jnp.zeros_like(low)

    @pl.when(jnp.logical_not(has_high))
    def _():
        high[...] = jnp.zeros_like(high)

    left_copy.wait()
    right_copy.wait()
    offsets_copy.wait()
    count = counts_ref[0]

    @pl.loop(0, slots)
    def _(slot):
        live = jnp.where(slot < count, 1.0, 0.0).astype(jnp.float32)
        left[slot] = (left[slot].astype(jnp.float32) * live).astype(left.dtype)
        right_t[pl.ds(pl.multiple_of(slot * width, width), width), :] = right[slot].T

    own_copy.wait()

    def gather(root):
        @pl.when(has_low)
        def _():
            up(root).wait_recv()

        @pl.when(has_high)
        def _():
            down(root).wait_recv()

        stage[0] = low[root]
        stage[1] = own[root]
        stage[2] = high[root]

    def settle(root):
        @pl.when(has_high)
        def _():
            up(root).wait_send()

        @pl.when(has_low)
        def _():
            down(root).wait_send()

        if rows:
            @pl.when(root < forwards)
            def _():
                forward(root, low, low_sem).wait_send()

    @pl.loop(0, roots - 1)
    def _(root):
        gather(root)
        total = apply_root(stage, offsets, left, right_t, mixed)
        out_ref[root] = total.astype(out_ref.dtype)

        if rows:
            @pl.when(root < forwards)
            def _():
                aside(root, root, 0, me).wait_recv()

                @pl.when(up_relay)
                def _():
                    forward(root, low, low_sem).start()

                @pl.when(down_relay)
                def _():
                    forward(root, high, high_sem).start()

        @pl.when(root >= 4)
        def _():
            settle(root - 4)

    gather(roots - 1)

    @pl.loop(roots - 5, roots)
    def _(root):
        settle(root)


def on_device(sectors, wave, left_ops, right_ops, deltas, counts):
    wave = wave[0]
    wave, left_ops, right_ops, deltas = (
        pltpu.with_memory_space_constraint(x, pltpu.HBM)
        for x in (wave, left_ops, right_ops, deltas)
    )
    roots, width = wave.shape[0], wave.shape[1]
    slots = left_ops.shape[0]
    block = (roots, width, width)
    bf16 = wave.dtype
    flops = 4 * roots * slots * width**3
    operand = (slots, width, width)
    operand_cat = (slots * width, width)
    held = pl.BlockSpec(memory_space=pltpu.VMEM)
    scalars = pl.BlockSpec(memory_space=pltpu.SMEM)
    done, left, right_t, stage, offsets = pl.pallas_call(
        functools.partial(kernel, sectors),
        out_shape=(
            pltpu.VMEM(block, bf16),
            pltpu.VMEM(operand, bf16),
            pltpu.VMEM(operand_cat, bf16),
            pltpu.VMEM((3, width, width), bf16),
            pltpu.SMEM(deltas.shape, deltas.dtype),
        ),
        in_specs=[scalars] + [pl.BlockSpec(memory_space=pltpu.HBM)] * 4,
        out_specs=(held, held, held, held, scalars),
        scratch_shapes=[
            pltpu.VMEM(block, bf16),
            pltpu.VMEM(block, bf16),
            pltpu.VMEM(block, bf16),
            pltpu.VMEM(block, bf16),
            pltpu.VMEM(operand, bf16),
            pltpu.VMEM((width, slots * width), bf16),
            pltpu.SemaphoreType.DMA((2, roots)),
            pltpu.SemaphoreType.DMA((roots,)),
            pltpu.SemaphoreType.DMA((roots,)),
            pltpu.SemaphoreType.DMA((roots,)),
            pltpu.SemaphoreType.DMA((roots,)),
            pltpu.SemaphoreType.DMA,
            pltpu.SemaphoreType.DMA((3,)),
        ],
        compiler_params=pltpu.CompilerParams(
            collective_id=0, has_side_effects=True, vmem_limit_bytes=48 * 2**20
        ),
        cost_estimate=pl.CostEstimate(flops=flops, bytes_accessed=7 * 2**20, transcendentals=0),
    )(counts, deltas, wave, left_ops, right_ops)
    sigma = pl.pallas_call(
        finish,
        out_shape=jax.ShapeDtypeStruct(block, bf16),
        in_specs=[scalars] + [held] * 4,
        out_specs=pl.BlockSpec(memory_space=pl.ANY),
        scratch_shapes=[
            pltpu.VMEM((width, slots * width), bf16),
            pltpu.VMEM((width, width), bf16),
            pltpu.SemaphoreType.DMA,
            pltpu.SemaphoreType.DMA,
        ],
        compiler_params=pltpu.CompilerParams(vmem_limit_bytes=48 * 2**20),
        cost_estimate=pl.CostEstimate(
            flops=flops // roots, bytes_accessed=2 * 2**20, transcendentals=0
        ),
    )(offsets, stage, left, right_t, done)
    return sigma[None]


def solution(mesh):
    return jax.shard_map(
        functools.partial(on_device, mesh.shape["sector"]),
        mesh=mesh,
        in_specs=(
            P(("group", "sector"), None, None, None),
            P(("group", "sector"), None, None),
            P(("group", "sector"), None, None),
            P(("group", "sector")),
            P(("group", "sector")),
        ),
        out_specs=P(("group", "sector"), None, None, None),
        check_vma=False,
    )
```

```python
import functools

import jax
import jax.numpy as jnp
from jax import lax
from jax.experimental import pallas as pl
from jax.experimental.pallas import tpu as pltpu
from jax.sharding import PartitionSpec as P

MESH = pl.DeviceIdType.MESH


def apply_root(stage, offsets, left, right_t, mixed):
    width = left.shape[1]
    slots = right_t.shape[0] // width
    for slot in range(slots):
        source = stage[offsets[slot] + 1]
        mixed[:, slot * width:(slot + 1) * width] = jnp.dot(
            left[slot], source, preferred_element_type=jnp.float32
        ).astype(mixed.dtype)
    return jnp.dot(mixed[...], right_t[...], preferred_element_type=jnp.float32)


def finish(
    reads, late, left, right_t, partial, done_ref, out_ref,
    order, mixed, total, result, done_sem, last_sem,
):
    last = out_ref.shape[0] - 1
    width = left.shape[1]
    slots = left.shape[0] - 1
    group = mixed.shape[1] // width
    done_copy = pltpu.make_async_copy(
        done_ref.at[pl.ds(0, last)], out_ref.at[pl.ds(0, last)], done_sem
    )
    done_copy.start()

    for place in range(slots + group):
        order[place] = slots
    found = jnp.int32(0)
    for slot in range(slots):
        order[found] = jnp.where(reads[slot] == 1, slot, slots)
        found = found + reads[slot]
    total[...] = partial[...]

    def add_group(step, carry):
        parts = None
        for place in range(group):
            slot = order[step * group + place]
            span = slice(place * width, (place + 1) * width)
            mixed[:, span] = jnp.dot(
                left[slot], late[...], preferred_element_type=jnp.float32
            ).astype(mixed.dtype)
            row = pl.multiple_of(jnp.minimum(slot, slots - 1) * width, width)
            part = jnp.dot(
                mixed[:, span], right_t[pl.ds(row, width), :], preferred_element_type=jnp.float32
            )
            parts = part if parts is None else parts + part
        total[...] += parts
        return carry

    lax.fori_loop(0, lax.div(found + group - 1, group), add_group, 0)
    result[...] = total[...].astype(result.dtype)
    last_copy = pltpu.make_async_copy(result, out_ref.at[last], last_sem)
    last_copy.start()
    done_copy.wait()
    last_copy.wait()


def kernel(
    sectors, counts_ref, deltas_ref, wave_ref, left_ref, right_ref,
    out_ref, left, right_t, late, partial, reads,
    own, low, high, passing, right, mixed, stage, offsets,
    send_sem, low_sem, high_sem, passing_sem, forward_sem, own_sem, op_sem,
):
    roots, width = own.shape[0], own.shape[1]
    slots = right.shape[0]
    last = roots - 1
    me = lax.axis_index("sector")
    has_low, has_high = me > 0, me < sectors - 1
    odd = lax.rem(me, 2) == 1

    rows = sectors // 4 if sectors == 16 else 0
    row, place = lax.div(me, 4), lax.rem(me, 4)
    above, below = row < rows - 1, jnp.logical_and(row > 0, row < rows)
    up_source = jnp.logical_and(place == 3, above)
    up_relay = jnp.logical_and(place == 1, above)
    down_source = jnp.logical_and(place == 0, below)
    down_relay = jnp.logical_and(place == 2, below)
    up_share = lax.div(roots * (rows - 1 - row), max(rows, 1))
    down_share = lax.div(roots * row, max(rows, 1))
    up_detour = jnp.where(up_source, up_share, 0)
    down_detour = jnp.where(down_source, down_share, 0)
    forwards = jnp.where(up_relay, up_share, jnp.where(down_relay, down_share, 0))
    ahead = jnp.where(up_relay, me + 3, jnp.where(down_relay, me - 3, me))

    partners = [(has_low, me - 1), (has_high, me + 1)]
    if rows:
        partners += [
            (up_source, me - 2), (up_source, me + 3),
            (down_source, me + 2), (down_source, me - 3),
            (up_relay, me + 2), (up_relay, me + 3),
            (down_relay, me - 2), (down_relay, me - 3),
        ]
    barrier = pltpu.get_barrier_semaphore()
    for present, partner in partners:
        @pl.when(present)
        def _(partner=partner):
            pl.semaphore_signal(barrier, inc=1, device_id={"sector": partner}, device_id_type=MESH)

    left_copy = pltpu.make_async_copy(left_ref, left.at[pl.ds(0, slots)], op_sem.at[0])
    right_copy = pltpu.make_async_copy(right_ref, right, op_sem.at[1])
    own_copy = pltpu.make_async_copy(wave_ref, own, own_sem)
    offsets_copy = pltpu.make_async_copy(deltas_ref, offsets, op_sem.at[2])
    offsets_copy.start()
    left_copy.start()
    right_copy.start()
    own_copy.start()
    pl.semaphore_wait(barrier, sum(present.astype(jnp.int32) for present, _ in partners))

    def up(root):
        return pltpu.make_async_remote_copy(
            src_ref=wave_ref.at[root], dst_ref=low.at[root],
            send_sem=send_sem.at[0, root], recv_sem=low_sem.at[root],
            device_id={"sector": me + 1}, device_id_type=MESH,
        )

    def down(root):
        return pltpu.make_async_remote_copy(
            src_ref=wave_ref.at[root], dst_ref=high.at[root],
            send_sem=send_sem.at[1, root], recv_sem=high_sem.at[root],
            device_id={"sector": me - 1}, device_id_type=MESH,
        )

    def aside(root, step, way, corner):
        return pltpu.make_async_remote_copy(
            src_ref=wave_ref.at[root], dst_ref=passing.at[step],
            send_sem=send_sem.at[way, root], recv_sem=passing_sem.at[step],
            device_id={"sector": corner}, device_id_type=MESH,
        )

    def forward(step, target, target_sem):
        root = roots - forwards + step
        return pltpu.make_async_remote_copy(
            src_ref=passing.at[step], dst_ref=target.at[root],
            send_sem=forward_sem.at[step], recv_sem=target_sem.at[root],
            device_id={"sector": ahead}, device_id_type=MESH,
        )

    @pl.loop(0, roots)
    def _(step):
        @pl.when(jnp.logical_and(has_high, step < roots - up_detour))
        def _():
            up(jnp.where(odd, step, lax.rem(step + last, roots))).start()

        @pl.when(jnp.logical_and(has_low, step < roots - down_detour))
        def _():
            down(jnp.where(odd, lax.rem(step + last, roots), step)).start()

        if rows:
            @pl.when(step < up_detour)
            def _():
                aside(roots - up_detour + step, step, 0, me - 2).start()

            @pl.when(step < down_detour)
            def _():
                aside(roots - down_detour + step, step, 1, me + 2).start()

    @pl.when(jnp.logical_not(has_low))
    def _():
        low[...] = jnp.zeros_like(low)

    @pl.when(jnp.logical_not(has_high))
    def _():
        high[...] = jnp.zeros_like(high)

    left_copy.wait()
    right_copy.wait()
    offsets_copy.wait()
    count = counts_ref[0]
    far = jnp.where(odd, 1, -1)
    left[slots] = jnp.zeros((width, width), left.dtype)

    @pl.loop(0, slots)
    def _(slot):
        live = jnp.where(slot < count, 1.0, 0.0).astype(jnp.float32)
        reads[slot] = jnp.where(
            jnp.logical_and(slot < count, offsets[slot] == far), 1, 0
        ).astype(jnp.int32)
        left[slot] = (left[slot].astype(jnp.float32) * live).astype(left.dtype)
        right_t[pl.ds(pl.multiple_of(slot * width, width), width), :] = right[slot].T

    own_copy.wait()

    def gather(root):
        @pl.when(has_low)
        def _():
            up(root).wait_recv()

        @pl.when(has_high)
        def _():
            down(root).wait_recv()

        stage[0] = low[root]
        stage[1] = own[root]
        stage[2] = high[root]

    def settle(root):
        @pl.when(has_high)
        def _():
            up(root).wait_send()

        @pl.when(has_low)
        def _():
            down(root).wait_send()

        if rows:
            @pl.when(root < forwards)
            def _():
                forward(root, low, low_sem).wait_send()

    @pl.when(odd)
    def _():
        up(last).wait_recv()
        stage[0] = low[last]
        stage[2] = jnp.zeros((width, width), stage.dtype)

    @pl.when(jnp.logical_not(odd))
    def _():
        down(last).wait_recv()
        stage[0] = jnp.zeros((width, width), stage.dtype)
        stage[2] = high[last]

    stage[1] = own[last]
    partial[...] = apply_root(stage, offsets, left, right_t, mixed)

    @pl.loop(0, last)
    def _(root):
        gather(root)
        total = apply_root(stage, offsets, left, right_t, mixed)
        out_ref[root] = total.astype(out_ref.dtype)

        if rows:
            @pl.when(root < forwards)
            def _():
                aside(root, root, 0, me).wait_recv()

                @pl.when(up_relay)
                def _():
                    forward(root, low, low_sem).start()

                @pl.when(down_relay)
                def _():
                    forward(root, high, high_sem).start()

        @pl.when(root >= 4)
        def _():
            settle(root - 4)

    @pl.when(odd)
    def _():
        @pl.when(has_high)
        def _():
            down(last).wait_recv()

        late[...] = high[last]

    @pl.when(jnp.logical_not(odd))
    def _():
        @pl.when(has_low)
        def _():
            up(last).wait_recv()

        late[...] = low[last]

    @pl.loop(roots - 5, roots)
    def _(root):
        settle(root)


def on_device(sectors, wave, left_ops, right_ops, deltas, counts):
    wave = wave[0]
    wave, left_ops, right_ops, deltas = (
        pltpu.with_memory_space_constraint(x, pltpu.HBM)
        for x in (wave, left_ops, right_ops, deltas)
    )
    roots, width = wave.shape[0], wave.shape[1]
    slots = left_ops.shape[0]
    block = (roots, width, width)
    bf16 = wave.dtype
    flops = 4 * roots * slots * width**3
    operand = (slots, width, width)
    operand_cat = (slots * width, width)
    held = pl.BlockSpec(memory_space=pltpu.VMEM)
    scalars = pl.BlockSpec(memory_space=pltpu.SMEM)
    done, left, right_t, late, partial, reads = pl.pallas_call(
        functools.partial(kernel, sectors),
        out_shape=(
            pltpu.VMEM(block, bf16),
            pltpu.VMEM((slots + 1, width, width), bf16),
            pltpu.VMEM(operand_cat, bf16),
            pltpu.VMEM((width, width), bf16),
            pltpu.VMEM((width, width), jnp.float32),
            pltpu.SMEM(deltas.shape, deltas.dtype),
        ),
        in_specs=[scalars] + [pl.BlockSpec(memory_space=pltpu.HBM)] * 4,
        out_specs=(held, held, held, held, held, scalars),
        scratch_shapes=[
            pltpu.VMEM(block, bf16),
            pltpu.VMEM(block, bf16),
            pltpu.VMEM(block, bf16),
            pltpu.VMEM(block, bf16),
            pltpu.VMEM(operand, bf16),
            pltpu.VMEM((width, slots * width), bf16),
            pltpu.VMEM((3, width, width), bf16),
            pltpu.SMEM(deltas.shape, deltas.dtype),
            pltpu.SemaphoreType.DMA((2, roots)),
            pltpu.SemaphoreType.DMA((roots,)),
            pltpu.SemaphoreType.DMA((roots,)),
            pltpu.SemaphoreType.DMA((roots,)),
            pltpu.SemaphoreType.DMA((roots,)),
            pltpu.SemaphoreType.DMA,
            pltpu.SemaphoreType.DMA((3,)),
        ],
        compiler_params=pltpu.CompilerParams(
            collective_id=0, has_side_effects=True, vmem_limit_bytes=48 * 2**20
        ),
        cost_estimate=pl.CostEstimate(flops=flops, bytes_accessed=7 * 2**20, transcendentals=0),
    )(counts, deltas, wave, left_ops, right_ops)
    sigma = pl.pallas_call(
        finish,
        out_shape=jax.ShapeDtypeStruct(block, bf16),
        in_specs=[scalars] + [held] * 5,
        out_specs=pl.BlockSpec(memory_space=pl.ANY),
        scratch_shapes=[
            pltpu.SMEM((slots + 3,), jnp.int32),
            pltpu.VMEM((width, 3 * width), bf16),
            pltpu.VMEM((width, width), jnp.float32),
            pltpu.VMEM((width, width), bf16),
            pltpu.SemaphoreType.DMA,
            pltpu.SemaphoreType.DMA,
        ],
        compiler_params=pltpu.CompilerParams(vmem_limit_bytes=48 * 2**20),
        cost_estimate=pl.CostEstimate(
            flops=flops // roots, bytes_accessed=2 * 2**20, transcendentals=0
        ),
    )(reads, late, left, right_t, partial, done)
    return sigma[None]


def solution(mesh):
    return jax.shard_map(
        functools.partial(on_device, mesh.shape["sector"]),
        mesh=mesh,
        in_specs=(
            P(("group", "sector"), None, None, None),
            P(("group", "sector"), None, None),
            P(("group", "sector"), None, None),
            P(("group", "sector")),
            P(("group", "sector")),
        ),
        out_specs=P(("group", "sector"), None, None, None),
        check_vma=False,
    )
```

```python
import functools

import jax
import jax.numpy as jnp
from jax import lax
from jax.experimental import pallas as pl
from jax.experimental.pallas import tpu as pltpu
from jax.sharding import PartitionSpec as P

MESH = pl.DeviceIdType.MESH


def apply_root(stage, offsets, left, right_t, mixed):
    width = left.shape[1]
    slots = right_t.shape[0] // width
    for slot in range(slots):
        source = stage[offsets[slot] + 1]
        mixed[:, slot * width:(slot + 1) * width] = jnp.dot(
            left[slot], source, preferred_element_type=jnp.float32
        ).astype(mixed.dtype)
    return jnp.dot(mixed[...], right_t[...], preferred_element_type=jnp.float32)


def finish(
    reads, late, left, right_t, partial, done_ref, out_ref,
    order, mixed, right, result, done_sem, last_sem,
):
    last = out_ref.shape[0] - 1
    width = left.shape[1]
    slots = left.shape[0] - 1
    done_copy = pltpu.make_async_copy(
        done_ref.at[pl.ds(0, last)], out_ref.at[pl.ds(0, last)], done_sem
    )
    done_copy.start()

    for place in range(slots):
        order[place] = slots
    found = jnp.int32(0)
    for slot in range(slots):
        order[found] = jnp.where(reads[slot] == 1, slot, slots)
        found = found + reads[slot]

    def add_late(size):
        for place in range(size):
            slot = order[place]
            span = slice(place * width, (place + 1) * width)
            row = pl.multiple_of(jnp.minimum(slot, slots - 1) * width, width)
            right[span, :] = right_t[pl.ds(row, width), :]
            mixed[:, span] = jnp.dot(
                left[slot], late[...], preferred_element_type=jnp.float32
            ).astype(mixed.dtype)
        depth = slice(0, size * width)
        added = jnp.dot(mixed[:, depth], right[depth, :], preferred_element_type=jnp.float32)
        result[...] = (partial[...] + added).astype(result.dtype)

    below = -1
    for size in sorted({-(-slots // 3), -(-2 * slots // 3), slots}):
        @pl.when(jnp.logical_and(found > below, found <= size))
        def _(size=size):
            add_late(size)

        below = size

    last_copy = pltpu.make_async_copy(result, out_ref.at[last], last_sem)
    last_copy.start()
    done_copy.wait()
    last_copy.wait()


def kernel(
    sectors, counts_ref, deltas_ref, wave_ref, left_ref, right_ref,
    out_ref, left, right_t, late, partial, reads,
    own, low, high, passing, right, mixed, stage, offsets,
    send_sem, low_sem, high_sem, passing_sem, forward_sem, own_sem, op_sem,
):
    roots, width = own.shape[0], own.shape[1]
    slots = right.shape[0]
    last = roots - 1
    me = lax.axis_index("sector")
    has_low, has_high = me > 0, me < sectors - 1
    odd = lax.rem(me, 2) == 1

    rows = sectors // 4 if sectors == 16 else 0
    row, place = lax.div(me, 4), lax.rem(me, 4)
    above, below = row < rows - 1, jnp.logical_and(row > 0, row < rows)
    up_source = jnp.logical_and(place == 3, above)
    up_relay = jnp.logical_and(place == 1, above)
    down_source = jnp.logical_and(place == 0, below)
    down_relay = jnp.logical_and(place == 2, below)
    up_share = lax.div(roots * (rows - 1 - row), max(rows, 1))
    down_share = lax.div(roots * row, max(rows, 1))
    up_detour = jnp.where(up_source, up_share, 0)
    down_detour = jnp.where(down_source, down_share, 0)
    forwards = jnp.where(up_relay, up_share, jnp.where(down_relay, down_share, 0))
    ahead = jnp.where(up_relay, me + 3, jnp.where(down_relay, me - 3, me))

    partners = [(has_low, me - 1), (has_high, me + 1)]
    if rows:
        partners += [
            (up_source, me - 2), (up_source, me + 3),
            (down_source, me + 2), (down_source, me - 3),
            (up_relay, me + 2), (up_relay, me + 3),
            (down_relay, me - 2), (down_relay, me - 3),
        ]
    barrier = pltpu.get_barrier_semaphore()
    for present, partner in partners:
        @pl.when(present)
        def _(partner=partner):
            pl.semaphore_signal(barrier, inc=1, device_id={"sector": partner}, device_id_type=MESH)

    left_copy = pltpu.make_async_copy(left_ref, left.at[pl.ds(0, slots)], op_sem.at[0])
    right_copy = pltpu.make_async_copy(right_ref, right, op_sem.at[1])
    own_copy = pltpu.make_async_copy(wave_ref, own, own_sem)
    offsets_copy = pltpu.make_async_copy(deltas_ref, offsets, op_sem.at[2])
    offsets_copy.start()
    left_copy.start()
    right_copy.start()
    own_copy.start()
    pl.semaphore_wait(barrier, sum(present.astype(jnp.int32) for present, _ in partners))

    def up(root):
        return pltpu.make_async_remote_copy(
            src_ref=wave_ref.at[root], dst_ref=low.at[root],
            send_sem=send_sem.at[0, root], recv_sem=low_sem.at[root],
            device_id={"sector": me + 1}, device_id_type=MESH,
        )

    def down(root):
        return pltpu.make_async_remote_copy(
            src_ref=wave_ref.at[root], dst_ref=high.at[root],
            send_sem=send_sem.at[1, root], recv_sem=high_sem.at[root],
            device_id={"sector": me - 1}, device_id_type=MESH,
        )

    def aside(root, step, way, corner):
        return pltpu.make_async_remote_copy(
            src_ref=wave_ref.at[root], dst_ref=passing.at[step],
            send_sem=send_sem.at[way, root], recv_sem=passing_sem.at[step],
            device_id={"sector": corner}, device_id_type=MESH,
        )

    def forward(step, target, target_sem):
        root = roots - forwards + step
        return pltpu.make_async_remote_copy(
            src_ref=passing.at[step], dst_ref=target.at[root],
            send_sem=forward_sem.at[step], recv_sem=target_sem.at[root],
            device_id={"sector": ahead}, device_id_type=MESH,
        )

    @pl.loop(0, roots)
    def _(step):
        @pl.when(jnp.logical_and(has_high, step < roots - up_detour))
        def _():
            up(jnp.where(odd, step, lax.rem(step + last, roots))).start()

        @pl.when(jnp.logical_and(has_low, step < roots - down_detour))
        def _():
            down(jnp.where(odd, lax.rem(step + last, roots), step)).start()

        if rows:
            @pl.when(step < up_detour)
            def _():
                aside(roots - up_detour + step, step, 0, me - 2).start()

            @pl.when(step < down_detour)
            def _():
                aside(roots - down_detour + step, step, 1, me + 2).start()

    @pl.when(jnp.logical_not(has_low))
    def _():
        low[...] = jnp.zeros_like(low)

    @pl.when(jnp.logical_not(has_high))
    def _():
        high[...] = jnp.zeros_like(high)

    left_copy.wait()
    right_copy.wait()
    offsets_copy.wait()
    count = counts_ref[0]
    far = jnp.where(odd, 1, -1)
    left[slots] = jnp.zeros((width, width), left.dtype)

    @pl.loop(0, slots)
    def _(slot):
        live = jnp.where(slot < count, 1.0, 0.0).astype(jnp.float32)
        reads[slot] = jnp.where(
            jnp.logical_and(slot < count, offsets[slot] == far), 1, 0
        ).astype(jnp.int32)
        left[slot] = (left[slot].astype(jnp.float32) * live).astype(left.dtype)
        right_t[pl.ds(pl.multiple_of(slot * width, width), width), :] = right[slot].T

    own_copy.wait()

    def gather(root):
        @pl.when(has_low)
        def _():
            up(root).wait_recv()

        @pl.when(has_high)
        def _():
            down(root).wait_recv()

        stage[0] = low[root]
        stage[1] = own[root]
        stage[2] = high[root]

    def settle(root):
        @pl.when(has_high)
        def _():
            up(root).wait_send()

        @pl.when(has_low)
        def _():
            down(root).wait_send()

        if rows:
            @pl.when(root < forwards)
            def _():
                forward(root, low, low_sem).wait_send()

    @pl.when(odd)
    def _():
        up(last).wait_recv()
        stage[0] = low[last]
        stage[2] = jnp.zeros((width, width), stage.dtype)

    @pl.when(jnp.logical_not(odd))
    def _():
        down(last).wait_recv()
        stage[0] = jnp.zeros((width, width), stage.dtype)
        stage[2] = high[last]

    stage[1] = own[last]
    partial[...] = apply_root(stage, offsets, left, right_t, mixed)

    @pl.loop(0, last)
    def _(root):
        gather(root)
        total = apply_root(stage, offsets, left, right_t, mixed)
        out_ref[root] = total.astype(out_ref.dtype)

        if rows:
            @pl.when(root < forwards)
            def _():
                aside(root, root, 0, me).wait_recv()

                @pl.when(up_relay)
                def _():
                    forward(root, low, low_sem).start()

                @pl.when(down_relay)
                def _():
                    forward(root, high, high_sem).start()

        @pl.when(root >= 4)
        def _():
            settle(root - 4)

    @pl.when(odd)
    def _():
        @pl.when(has_high)
        def _():
            down(last).wait_recv()

        late[...] = high[last]

    @pl.when(jnp.logical_not(odd))
    def _():
        @pl.when(has_low)
        def _():
            up(last).wait_recv()

        late[...] = low[last]

    @pl.loop(roots - 5, roots)
    def _(root):
        settle(root)


def on_device(sectors, wave, left_ops, right_ops, deltas, counts):
    wave = wave[0]
    wave, left_ops, right_ops, deltas = (
        pltpu.with_memory_space_constraint(x, pltpu.HBM)
        for x in (wave, left_ops, right_ops, deltas)
    )
    roots, width = wave.shape[0], wave.shape[1]
    slots = left_ops.shape[0]
    block = (roots, width, width)
    bf16 = wave.dtype
    flops = 4 * roots * slots * width**3
    operand = (slots, width, width)
    operand_cat = (slots * width, width)
    held = pl.BlockSpec(memory_space=pltpu.VMEM)
    scalars = pl.BlockSpec(memory_space=pltpu.SMEM)
    done, left, right_t, late, partial, reads = pl.pallas_call(
        functools.partial(kernel, sectors),
        out_shape=(
            pltpu.VMEM(block, bf16),
            pltpu.VMEM((slots + 1, width, width), bf16),
            pltpu.VMEM(operand_cat, bf16),
            pltpu.VMEM((width, width), bf16),
            pltpu.VMEM((width, width), jnp.float32),
            pltpu.SMEM(deltas.shape, deltas.dtype),
        ),
        in_specs=[scalars] + [pl.BlockSpec(memory_space=pltpu.HBM)] * 4,
        out_specs=(held, held, held, held, held, scalars),
        scratch_shapes=[
            pltpu.VMEM(block, bf16),
            pltpu.VMEM(block, bf16),
            pltpu.VMEM(block, bf16),
            pltpu.VMEM(block, bf16),
            pltpu.VMEM(operand, bf16),
            pltpu.VMEM((width, slots * width), bf16),
            pltpu.VMEM((3, width, width), bf16),
            pltpu.SMEM(deltas.shape, deltas.dtype),
            pltpu.SemaphoreType.DMA((2, roots)),
            pltpu.SemaphoreType.DMA((roots,)),
            pltpu.SemaphoreType.DMA((roots,)),
            pltpu.SemaphoreType.DMA((roots,)),
            pltpu.SemaphoreType.DMA((roots,)),
            pltpu.SemaphoreType.DMA,
            pltpu.SemaphoreType.DMA((3,)),
        ],
        compiler_params=pltpu.CompilerParams(
            collective_id=0, has_side_effects=True, vmem_limit_bytes=48 * 2**20
        ),
        cost_estimate=pl.CostEstimate(flops=flops, bytes_accessed=7 * 2**20, transcendentals=0),
    )(counts, deltas, wave, left_ops, right_ops)
    sigma = pl.pallas_call(
        finish,
        out_shape=jax.ShapeDtypeStruct(block, bf16),
        in_specs=[scalars] + [held] * 5,
        out_specs=pl.BlockSpec(memory_space=pl.ANY),
        scratch_shapes=[
            pltpu.SMEM((slots,), jnp.int32),
            pltpu.VMEM((width, slots * width), bf16),
            pltpu.VMEM((slots * width, width), bf16),
            pltpu.VMEM((width, width), bf16),
            pltpu.SemaphoreType.DMA,
            pltpu.SemaphoreType.DMA,
        ],
        compiler_params=pltpu.CompilerParams(vmem_limit_bytes=48 * 2**20),
        cost_estimate=pl.CostEstimate(
            flops=flops // roots, bytes_accessed=2 * 2**20, transcendentals=0
        ),
    )(reads, late, left, right_t, partial, done)
    return sigma[None]


def solution(mesh):
    return jax.shard_map(
        functools.partial(on_device, mesh.shape["sector"]),
        mesh=mesh,
        in_specs=(
            P(("group", "sector"), None, None, None),
            P(("group", "sector"), None, None),
            P(("group", "sector"), None, None),
            P(("group", "sector")),
            P(("group", "sector")),
        ),
        out_specs=P(("group", "sector"), None, None, None),
        check_vma=False,
    )
```

```python
import functools

import jax
import jax.numpy as jnp
from jax import lax
from jax.experimental import pallas as pl
from jax.experimental.pallas import tpu as pltpu
from jax.sharding import PartitionSpec as P

MESH = pl.DeviceIdType.MESH


def apply_root(stage, offsets, left, right_t, mixed):
    width = left.shape[1]
    slots = right_t.shape[0] // width
    for slot in range(slots):
        source = stage[offsets[slot] + 1]
        mixed[:, slot * width:(slot + 1) * width] = jnp.dot(
            left[slot], source, preferred_element_type=jnp.float32
        ).astype(mixed.dtype)
    return jnp.dot(mixed[...], right_t[...], preferred_element_type=jnp.float32)


def finish(
    reads, late, left, right_t, partial, done_ref, out_ref,
    order, mixed, right, result, done_sem, last_sem,
):
    last = out_ref.shape[0] - 1
    width = left.shape[1]
    slots = left.shape[0] - 1
    pieces = done_sem.shape[0]
    edges = [last * piece // pieces for piece in range(pieces + 1)]
    done_copies = [
        pltpu.make_async_copy(
            done_ref.at[pl.ds(start, stop - start)], out_ref.at[pl.ds(start, stop - start)],
            done_sem.at[piece],
        )
        for piece, (start, stop) in enumerate(zip(edges, edges[1:]))
    ]
    for copy in done_copies:
        copy.start()

    for place in range(slots):
        order[place] = slots
    found = jnp.int32(0)
    for slot in range(slots):
        order[found] = jnp.where(reads[slot] == 1, slot, slots)
        found = found + reads[slot]

    def add_late(size):
        for place in range(size):
            slot = order[place]
            span = slice(place * width, (place + 1) * width)
            row = pl.multiple_of(jnp.minimum(slot, slots - 1) * width, width)
            right[span, :] = right_t[pl.ds(row, width), :]
            mixed[:, span] = jnp.dot(
                left[slot], late[...], preferred_element_type=jnp.float32
            ).astype(mixed.dtype)
        depth = slice(0, size * width)
        added = jnp.dot(mixed[:, depth], right[depth, :], preferred_element_type=jnp.float32)
        result[...] = (partial[...] + added).astype(result.dtype)

    below = -1
    for size in sorted({-(-slots // 3), -(-2 * slots // 3), slots}):
        @pl.when(jnp.logical_and(found > below, found <= size))
        def _(size=size):
            add_late(size)

        below = size

    last_copy = pltpu.make_async_copy(result, out_ref.at[last], last_sem)
    last_copy.start()
    for copy in done_copies:
        copy.wait()
    last_copy.wait()


def kernel(
    sectors, counts_ref, deltas_ref, wave_ref, left_ref, right_ref,
    out_ref, left, right_t, late, partial, reads,
    own, low, high, passing, right, mixed, stage, offsets,
    send_sem, low_sem, high_sem, passing_sem, forward_sem, own_sem, op_sem,
):
    roots, width = own.shape[0], own.shape[1]
    slots = right.shape[0]
    last = roots - 1
    me = lax.axis_index("sector")
    has_low, has_high = me > 0, me < sectors - 1
    odd = lax.rem(me, 2) == 1

    rows = sectors // 4 if sectors == 16 else 0
    row, place = lax.div(me, 4), lax.rem(me, 4)
    above, below = row < rows - 1, jnp.logical_and(row > 0, row < rows)
    up_source = jnp.logical_and(place == 3, above)
    up_relay = jnp.logical_and(place == 1, above)
    down_source = jnp.logical_and(place == 0, below)
    down_relay = jnp.logical_and(place == 2, below)
    up_share = lax.div(roots * (rows - 1 - row), max(rows, 1))
    down_share = lax.div(roots * row, max(rows, 1))
    up_detour = jnp.where(up_source, up_share, 0)
    down_detour = jnp.where(down_source, down_share, 0)
    forwards = jnp.where(up_relay, up_share, jnp.where(down_relay, down_share, 0))
    ahead = jnp.where(up_relay, me + 3, jnp.where(down_relay, me - 3, me))

    partners = [(has_low, me - 1), (has_high, me + 1)]
    if rows:
        partners += [
            (up_source, me - 2), (up_source, me + 3),
            (down_source, me + 2), (down_source, me - 3),
            (up_relay, me + 2), (up_relay, me + 3),
            (down_relay, me - 2), (down_relay, me - 3),
        ]
    barrier = pltpu.get_barrier_semaphore()
    for present, partner in partners:
        @pl.when(present)
        def _(partner=partner):
            pl.semaphore_signal(barrier, inc=1, device_id={"sector": partner}, device_id_type=MESH)

    left_copy = pltpu.make_async_copy(left_ref, left.at[pl.ds(0, slots)], op_sem.at[0])
    right_copy = pltpu.make_async_copy(right_ref, right, op_sem.at[1])
    own_copy = pltpu.make_async_copy(wave_ref, own, own_sem)
    offsets_copy = pltpu.make_async_copy(deltas_ref, offsets, op_sem.at[2])
    offsets_copy.start()
    left_copy.start()
    right_copy.start()
    own_copy.start()
    pl.semaphore_wait(barrier, sum(present.astype(jnp.int32) for present, _ in partners))

    def up(root):
        return pltpu.make_async_remote_copy(
            src_ref=wave_ref.at[root], dst_ref=low.at[root],
            send_sem=send_sem.at[0, root], recv_sem=low_sem.at[root],
            device_id={"sector": me + 1}, device_id_type=MESH,
        )

    def down(root):
        return pltpu.make_async_remote_copy(
            src_ref=wave_ref.at[root], dst_ref=high.at[root],
            send_sem=send_sem.at[1, root], recv_sem=high_sem.at[root],
            device_id={"sector": me - 1}, device_id_type=MESH,
        )

    def aside(root, step, way, corner):
        return pltpu.make_async_remote_copy(
            src_ref=wave_ref.at[root], dst_ref=passing.at[step],
            send_sem=send_sem.at[way, root], recv_sem=passing_sem.at[step],
            device_id={"sector": corner}, device_id_type=MESH,
        )

    def forward(step, target, target_sem):
        root = roots - forwards + step
        return pltpu.make_async_remote_copy(
            src_ref=passing.at[step], dst_ref=target.at[root],
            send_sem=forward_sem.at[step], recv_sem=target_sem.at[root],
            device_id={"sector": ahead}, device_id_type=MESH,
        )

    @pl.loop(0, roots)
    def _(step):
        @pl.when(jnp.logical_and(has_high, step < roots - up_detour))
        def _():
            up(jnp.where(odd, step, lax.rem(step + last, roots))).start()

        @pl.when(jnp.logical_and(has_low, step < roots - down_detour))
        def _():
            down(jnp.where(odd, lax.rem(step + last, roots), step)).start()

        if rows:
            @pl.when(step < up_detour)
            def _():
                aside(roots - up_detour + step, step, 0, me - 2).start()

            @pl.when(step < down_detour)
            def _():
                aside(roots - down_detour + step, step, 1, me + 2).start()

    @pl.when(jnp.logical_not(has_low))
    def _():
        low[...] = jnp.zeros_like(low)

    @pl.when(jnp.logical_not(has_high))
    def _():
        high[...] = jnp.zeros_like(high)

    left_copy.wait()
    right_copy.wait()
    offsets_copy.wait()
    count = counts_ref[0]
    far = jnp.where(odd, 1, -1)
    left[slots] = jnp.zeros((width, width), left.dtype)

    @pl.loop(0, slots)
    def _(slot):
        live = jnp.where(slot < count, 1.0, 0.0).astype(jnp.float32)
        reads[slot] = jnp.where(
            jnp.logical_and(slot < count, offsets[slot] == far), 1, 0
        ).astype(jnp.int32)
        left[slot] = (left[slot].astype(jnp.float32) * live).astype(left.dtype)
        right_t[pl.ds(pl.multiple_of(slot * width, width), width), :] = right[slot].T

    own_copy.wait()

    def gather(root):
        @pl.when(has_low)
        def _():
            up(root).wait_recv()

        @pl.when(has_high)
        def _():
            down(root).wait_recv()

        stage[0] = low[root]
        stage[1] = own[root]
        stage[2] = high[root]

    def settle(root):
        @pl.when(has_high)
        def _():
            up(root).wait_send()

        @pl.when(has_low)
        def _():
            down(root).wait_send()

        if rows:
            @pl.when(root < forwards)
            def _():
                forward(root, low, low_sem).wait_send()

    @pl.when(odd)
    def _():
        up(last).wait_recv()
        stage[0] = low[last]
        stage[2] = jnp.zeros((width, width), stage.dtype)

    @pl.when(jnp.logical_not(odd))
    def _():
        down(last).wait_recv()
        stage[0] = jnp.zeros((width, width), stage.dtype)
        stage[2] = high[last]

    stage[1] = own[last]
    partial[...] = apply_root(stage, offsets, left, right_t, mixed)

    @pl.loop(0, last)
    def _(root):
        gather(root)
        total = apply_root(stage, offsets, left, right_t, mixed)
        out_ref[root] = total.astype(out_ref.dtype)

        if rows:
            @pl.when(root < forwards)
            def _():
                aside(root, root, 0, me).wait_recv()

                @pl.when(up_relay)
                def _():
                    forward(root, low, low_sem).start()

                @pl.when(down_relay)
                def _():
                    forward(root, high, high_sem).start()

        @pl.when(root >= 4)
        def _():
            settle(root - 4)

    @pl.when(odd)
    def _():
        @pl.when(has_high)
        def _():
            down(last).wait_recv()

        late[...] = high[last]

    @pl.when(jnp.logical_not(odd))
    def _():
        @pl.when(has_low)
        def _():
            up(last).wait_recv()

        late[...] = low[last]

    @pl.loop(roots - 5, roots)
    def _(root):
        settle(root)


def on_device(sectors, wave, left_ops, right_ops, deltas, counts):
    wave = wave[0]
    wave, left_ops, right_ops, deltas = (
        pltpu.with_memory_space_constraint(x, pltpu.HBM)
        for x in (wave, left_ops, right_ops, deltas)
    )
    roots, width = wave.shape[0], wave.shape[1]
    slots = left_ops.shape[0]
    block = (roots, width, width)
    bf16 = wave.dtype
    flops = 4 * roots * slots * width**3
    operand = (slots, width, width)
    operand_cat = (slots * width, width)
    held = pl.BlockSpec(memory_space=pltpu.VMEM)
    scalars = pl.BlockSpec(memory_space=pltpu.SMEM)
    done, left, right_t, late, partial, reads = pl.pallas_call(
        functools.partial(kernel, sectors),
        out_shape=(
            pltpu.VMEM(block, bf16),
            pltpu.VMEM((slots + 1, width, width), bf16),
            pltpu.VMEM(operand_cat, bf16),
            pltpu.VMEM((width, width), bf16),
            pltpu.VMEM((width, width), jnp.float32),
            pltpu.SMEM(deltas.shape, deltas.dtype),
        ),
        in_specs=[scalars] + [pl.BlockSpec(memory_space=pltpu.HBM)] * 4,
        out_specs=(held, held, held, held, held, scalars),
        scratch_shapes=[
            pltpu.VMEM(block, bf16),
            pltpu.VMEM(block, bf16),
            pltpu.VMEM(block, bf16),
            pltpu.VMEM(block, bf16),
            pltpu.VMEM(operand, bf16),
            pltpu.VMEM((width, slots * width), bf16),
            pltpu.VMEM((3, width, width), bf16),
            pltpu.SMEM(deltas.shape, deltas.dtype),
            pltpu.SemaphoreType.DMA((2, roots)),
            pltpu.SemaphoreType.DMA((roots,)),
            pltpu.SemaphoreType.DMA((roots,)),
            pltpu.SemaphoreType.DMA((roots,)),
            pltpu.SemaphoreType.DMA((roots,)),
            pltpu.SemaphoreType.DMA,
            pltpu.SemaphoreType.DMA((3,)),
        ],
        compiler_params=pltpu.CompilerParams(
            collective_id=0, has_side_effects=True, vmem_limit_bytes=48 * 2**20
        ),
        cost_estimate=pl.CostEstimate(flops=flops, bytes_accessed=7 * 2**20, transcendentals=0),
    )(counts, deltas, wave, left_ops, right_ops)
    sigma = pl.pallas_call(
        finish,
        out_shape=jax.ShapeDtypeStruct(block, bf16),
        in_specs=[scalars] + [held] * 5,
        out_specs=pl.BlockSpec(memory_space=pl.ANY),
        scratch_shapes=[
            pltpu.SMEM((slots,), jnp.int32),
            pltpu.VMEM((width, slots * width), bf16),
            pltpu.VMEM((slots * width, width), bf16),
            pltpu.VMEM((width, width), bf16),
            pltpu.SemaphoreType.DMA((5,)),
            pltpu.SemaphoreType.DMA,
        ],
        compiler_params=pltpu.CompilerParams(vmem_limit_bytes=48 * 2**20),
        cost_estimate=pl.CostEstimate(
            flops=flops // roots, bytes_accessed=2 * 2**20, transcendentals=0
        ),
    )(reads, late, left, right_t, partial, done)
    return sigma[None]


def solution(mesh):
    return jax.shard_map(
        functools.partial(on_device, mesh.shape["sector"]),
        mesh=mesh,
        in_specs=(
            P(("group", "sector"), None, None, None),
            P(("group", "sector"), None, None),
            P(("group", "sector"), None, None),
            P(("group", "sector")),
            P(("group", "sector")),
        ),
        out_specs=P(("group", "sector"), None, None, None),
        check_vma=False,
    )
```

```python
import functools

import jax
import jax.numpy as jnp
from jax import lax
from jax.experimental import pallas as pl
from jax.experimental.pallas import tpu as pltpu
from jax.sharding import PartitionSpec as P

MESH = pl.DeviceIdType.MESH


def apply_root(stage, offsets, left, right_t, mixed):
    width = left.shape[1]
    slots = right_t.shape[0] // width
    for slot in range(slots):
        source = stage[offsets[slot] + 1]
        mixed[:, slot * width:(slot + 1) * width] = jnp.dot(
            left[slot], source, preferred_element_type=jnp.float32
        ).astype(mixed.dtype)
    return jnp.dot(mixed[...], right_t[...], preferred_element_type=jnp.float32)


def finish(
    reads, late, left, right_t, partial, done_ref, out_ref,
    order, mixed, right, result, done_sem, last_sem,
):
    last = out_ref.shape[0] - 1
    width = left.shape[1]
    slots = left.shape[0] - 1
    pieces = done_sem.shape[0]
    edges = [last * piece // pieces for piece in range(pieces + 1)]
    done_copies = [
        pltpu.make_async_copy(
            done_ref.at[pl.ds(start, stop - start)], out_ref.at[pl.ds(start, stop - start)],
            done_sem.at[piece],
        )
        for piece, (start, stop) in enumerate(zip(edges, edges[1:]))
    ]
    for copy in done_copies:
        copy.start()

    for place in range(slots):
        order[place] = slots
    found = jnp.int32(0)
    for slot in range(slots):
        order[found] = jnp.where(reads[slot] == 1, slot, slots)
        found = found + reads[slot]

    def add_late(size):
        for place in range(size):
            slot = order[place]
            span = slice(place * width, (place + 1) * width)
            row = pl.multiple_of(jnp.minimum(slot, slots - 1) * width, width)
            right[span, :] = right_t[pl.ds(row, width), :]
            mixed[:, span] = jnp.dot(
                left[slot], late[...], preferred_element_type=jnp.float32
            ).astype(mixed.dtype)
        depth = slice(0, size * width)
        added = jnp.dot(mixed[:, depth], right[depth, :], preferred_element_type=jnp.float32)
        result[...] = (partial[...] + added).astype(result.dtype)

    below = -1
    for size in sorted({-(-slots // 3), -(-2 * slots // 3), slots}):
        @pl.when(jnp.logical_and(found > below, found <= size))
        def _(size=size):
            add_late(size)

        below = size

    last_copy = pltpu.make_async_copy(result, out_ref.at[last], last_sem)
    last_copy.start()
    for copy in done_copies:
        copy.wait()
    last_copy.wait()


def kernel(
    sectors, counts_ref, deltas_ref, wave_ref, left_ref, right_ref,
    out_ref, left, right_t, late, partial, reads,
    own, low, high, passing, right, mixed, stage, offsets,
    send_sem, low_sem, high_sem, passing_sem, forward_sem, own_sem, op_sem,
):
    roots, width = own.shape[0], own.shape[1]
    slots = right.shape[0]
    last = roots - 1
    me = lax.axis_index("sector")
    has_low, has_high = me > 0, me < sectors - 1
    odd = lax.rem(me, 2) == 1

    rows = sectors // 4 if sectors == 16 else 0
    row, place = lax.div(me, 4), lax.rem(me, 4)
    above, below = row < rows - 1, jnp.logical_and(row > 0, row < rows)
    up_source = jnp.logical_and(place == 3, above)
    up_relay = jnp.logical_and(place == 0, above)
    down_source = jnp.logical_and(place == 0, below)
    down_relay = jnp.logical_and(place == 3, below)
    up_share = lax.div(roots * (rows - 1 - row), max(rows, 1))
    down_share = lax.div(roots * row, max(rows, 1))
    up_detour = jnp.where(up_source, up_share, 0)
    down_detour = jnp.where(down_source, down_share, 0)
    forwards = jnp.where(up_relay, up_share, jnp.where(down_relay, down_share, 0))
    ahead = jnp.where(up_relay, me + 4, jnp.where(down_relay, me - 4, me))

    partners = [(has_low, me - 1), (has_high, me + 1)]
    if rows:
        partners += [
            (up_source, me - 3), (up_source, me + 4),
            (down_source, me + 3), (down_source, me - 4),
            (up_relay, me + 3), (up_relay, me + 4),
            (down_relay, me - 3), (down_relay, me - 4),
        ]
    barrier = pltpu.get_barrier_semaphore()
    for present, partner in partners:
        @pl.when(present)
        def _(partner=partner):
            pl.semaphore_signal(barrier, inc=1, device_id={"sector": partner}, device_id_type=MESH)

    left_copy = pltpu.make_async_copy(left_ref, left.at[pl.ds(0, slots)], op_sem.at[0])
    right_copy = pltpu.make_async_copy(right_ref, right, op_sem.at[1])
    own_copy = pltpu.make_async_copy(wave_ref, own, own_sem)
    offsets_copy = pltpu.make_async_copy(deltas_ref, offsets, op_sem.at[2])
    offsets_copy.start()
    left_copy.start()
    right_copy.start()
    own_copy.start()
    pl.semaphore_wait(barrier, sum(present.astype(jnp.int32) for present, _ in partners))

    def up(root):
        return pltpu.make_async_remote_copy(
            src_ref=wave_ref.at[root], dst_ref=low.at[root],
            send_sem=send_sem.at[0, root], recv_sem=low_sem.at[root],
            device_id={"sector": me + 1}, device_id_type=MESH,
        )

    def down(root):
        return pltpu.make_async_remote_copy(
            src_ref=wave_ref.at[root], dst_ref=high.at[root],
            send_sem=send_sem.at[1, root], recv_sem=high_sem.at[root],
            device_id={"sector": me - 1}, device_id_type=MESH,
        )

    def aside(root, step, way, corner):
        return pltpu.make_async_remote_copy(
            src_ref=wave_ref.at[root], dst_ref=passing.at[step],
            send_sem=send_sem.at[way, root], recv_sem=passing_sem.at[step],
            device_id={"sector": corner}, device_id_type=MESH,
        )

    def forward(step, target, target_sem):
        root = roots - forwards + step
        return pltpu.make_async_remote_copy(
            src_ref=passing.at[step], dst_ref=target.at[root],
            send_sem=forward_sem.at[step], recv_sem=target_sem.at[root],
            device_id={"sector": ahead}, device_id_type=MESH,
        )

    @pl.loop(0, roots)
    def _(step):
        @pl.when(jnp.logical_and(has_high, step < roots - up_detour))
        def _():
            up(jnp.where(odd, step, lax.rem(step + last, roots))).start()

        @pl.when(jnp.logical_and(has_low, step < roots - down_detour))
        def _():
            down(jnp.where(odd, lax.rem(step + last, roots), step)).start()

        if rows:
            @pl.when(step < up_detour)
            def _():
                aside(roots - up_detour + step, step, 0, me - 3).start()

            @pl.when(step < down_detour)
            def _():
                aside(roots - down_detour + step, step, 1, me + 3).start()

    @pl.when(jnp.logical_not(has_low))
    def _():
        low[...] = jnp.zeros_like(low)

    @pl.when(jnp.logical_not(has_high))
    def _():
        high[...] = jnp.zeros_like(high)

    left_copy.wait()
    right_copy.wait()
    offsets_copy.wait()
    count = counts_ref[0]
    far = jnp.where(odd, 1, -1)
    left[slots] = jnp.zeros((width, width), left.dtype)

    @pl.loop(0, slots)
    def _(slot):
        live = jnp.where(slot < count, 1.0, 0.0).astype(jnp.float32)
        reads[slot] = jnp.where(
            jnp.logical_and(slot < count, offsets[slot] == far), 1, 0
        ).astype(jnp.int32)
        left[slot] = (left[slot].astype(jnp.float32) * live).astype(left.dtype)
        right_t[pl.ds(pl.multiple_of(slot * width, width), width), :] = right[slot].T

    own_copy.wait()

    def gather(root):
        @pl.when(has_low)
        def _():
            up(root).wait_recv()

        @pl.when(has_high)
        def _():
            down(root).wait_recv()

        stage[0] = low[root]
        stage[1] = own[root]
        stage[2] = high[root]

    def settle(root):
        @pl.when(has_high)
        def _():
            up(root).wait_send()

        @pl.when(has_low)
        def _():
            down(root).wait_send()

        if rows:
            @pl.when(root < forwards)
            def _():
                forward(root, low, low_sem).wait_send()

    @pl.when(odd)
    def _():
        up(last).wait_recv()
        stage[0] = low[last]
        stage[2] = jnp.zeros((width, width), stage.dtype)

    @pl.when(jnp.logical_not(odd))
    def _():
        down(last).wait_recv()
        stage[0] = jnp.zeros((width, width), stage.dtype)
        stage[2] = high[last]

    stage[1] = own[last]
    partial[...] = apply_root(stage, offsets, left, right_t, mixed)

    @pl.loop(0, last)
    def _(root):
        gather(root)
        total = apply_root(stage, offsets, left, right_t, mixed)
        out_ref[root] = total.astype(out_ref.dtype)

        if rows:
            @pl.when(root < forwards)
            def _():
                aside(root, root, 0, me).wait_recv()

                @pl.when(up_relay)
                def _():
                    forward(root, low, low_sem).start()

                @pl.when(down_relay)
                def _():
                    forward(root, high, high_sem).start()

        @pl.when(root >= 4)
        def _():
            settle(root - 4)

    @pl.when(odd)
    def _():
        @pl.when(has_high)
        def _():
            down(last).wait_recv()

        late[...] = high[last]

    @pl.when(jnp.logical_not(odd))
    def _():
        @pl.when(has_low)
        def _():
            up(last).wait_recv()

        late[...] = low[last]

    @pl.loop(roots - 5, roots)
    def _(root):
        settle(root)


def on_device(sectors, wave, left_ops, right_ops, deltas, counts):
    wave = wave[0]
    wave, left_ops, right_ops, deltas = (
        pltpu.with_memory_space_constraint(x, pltpu.HBM)
        for x in (wave, left_ops, right_ops, deltas)
    )
    roots, width = wave.shape[0], wave.shape[1]
    slots = left_ops.shape[0]
    block = (roots, width, width)
    bf16 = wave.dtype
    flops = 4 * roots * slots * width**3
    operand = (slots, width, width)
    operand_cat = (slots * width, width)
    held = pl.BlockSpec(memory_space=pltpu.VMEM)
    scalars = pl.BlockSpec(memory_space=pltpu.SMEM)
    done, left, right_t, late, partial, reads = pl.pallas_call(
        functools.partial(kernel, sectors),
        out_shape=(
            pltpu.VMEM(block, bf16),
            pltpu.VMEM((slots + 1, width, width), bf16),
            pltpu.VMEM(operand_cat, bf16),
            pltpu.VMEM((width, width), bf16),
            pltpu.VMEM((width, width), jnp.float32),
            pltpu.SMEM(deltas.shape, deltas.dtype),
        ),
        in_specs=[scalars] + [pl.BlockSpec(memory_space=pltpu.HBM)] * 4,
        out_specs=(held, held, held, held, held, scalars),
        scratch_shapes=[
            pltpu.VMEM(block, bf16),
            pltpu.VMEM(block, bf16),
            pltpu.VMEM(block, bf16),
            pltpu.VMEM(block, bf16),
            pltpu.VMEM(operand, bf16),
            pltpu.VMEM((width, slots * width), bf16),
            pltpu.VMEM((3, width, width), bf16),
            pltpu.SMEM(deltas.shape, deltas.dtype),
            pltpu.SemaphoreType.DMA((2, roots)),
            pltpu.SemaphoreType.DMA((roots,)),
            pltpu.SemaphoreType.DMA((roots,)),
            pltpu.SemaphoreType.DMA((roots,)),
            pltpu.SemaphoreType.DMA((roots,)),
            pltpu.SemaphoreType.DMA,
            pltpu.SemaphoreType.DMA((3,)),
        ],
        compiler_params=pltpu.CompilerParams(
            collective_id=0, has_side_effects=True, vmem_limit_bytes=48 * 2**20
        ),
        cost_estimate=pl.CostEstimate(flops=flops, bytes_accessed=7 * 2**20, transcendentals=0),
    )(counts, deltas, wave, left_ops, right_ops)
    sigma = pl.pallas_call(
        finish,
        out_shape=jax.ShapeDtypeStruct(block, bf16),
        in_specs=[scalars] + [held] * 5,
        out_specs=pl.BlockSpec(memory_space=pl.ANY),
        scratch_shapes=[
            pltpu.SMEM((slots,), jnp.int32),
            pltpu.VMEM((width, slots * width), bf16),
            pltpu.VMEM((slots * width, width), bf16),
            pltpu.VMEM((width, width), bf16),
            pltpu.SemaphoreType.DMA((5,)),
            pltpu.SemaphoreType.DMA,
        ],
        compiler_params=pltpu.CompilerParams(vmem_limit_bytes=48 * 2**20),
        cost_estimate=pl.CostEstimate(
            flops=flops // roots, bytes_accessed=2 * 2**20, transcendentals=0
        ),
    )(reads, late, left, right_t, partial, done)
    return sigma[None]


def solution(mesh):
    return jax.shard_map(
        functools.partial(on_device, mesh.shape["sector"]),
        mesh=mesh,
        in_specs=(
            P(("group", "sector"), None, None, None),
            P(("group", "sector"), None, None),
            P(("group", "sector"), None, None),
            P(("group", "sector")),
            P(("group", "sector")),
        ),
        out_specs=P(("group", "sector"), None, None, None),
        check_vma=False,
    )
```
